256 devices in a mesh: gx: 4 (over x_hi, core), gy: 4 (over y), gz: 16 (over x_lo, z).
Axes of the slice: x: 4 (x_hi: 2, x_lo: 2; x = x_hi * 2 + x_lo), y: 4, z: 8, core: 2. Of those that a mesh axis runs over, the one named last changes fastest.
Arguments:
- tokens: bfloat16 [1024, 6144], P(('gx', 'gy'), 'gz'), may hold values from -6 to 6
- w_up: bfloat16 [6144, 24576], P('gz', ('gx', 'gy')), may hold values from -0.109375 to 0.109375
- b_up: float32 [24576], P(('gx', 'gz')), may hold values from -3 to 3
- w_down: bfloat16 [24576, 6144], P(('gx', 'gy'), 'gz'), may hold values from -0.0546875 to 0.0546875
- b_down: float32 [6144], P('gz'), may hold values from -3 to 3
- cotangent: bfloat16 [1024, 6144], P(('gx', 'gy'), 'gz'), may hold values from -1.5 to 1.5
Outputs:
- output: bfloat16 [1024, 6144], P(('gx', 'gy'), 'gz')
- grad_tokens: bfloat16 [1024, 6144], P(('gx', 'gy'), 'gz')
- grad_w_up: bfloat16 [6144, 24576], P('gz', ('gx', 'gy'))
- grad_b_up: float32 [24576], P(('gx', 'gz'))
- grad_w_down: bfloat16 [24576, 6144], P(('gx', 'gy'), 'gz')
- grad_b_down: float32 [6144], P('gz')
The draws below stay inside these ranges and needn't reach their ends.
All inputs are finite; a program needn't handle non-finite values.
Results may differ from the reference program's by a relative error of at most 0.033.
Values may be sent and summed in bfloat16 or wider, within the bound.
A program may use at most 128 MiB of HBM per device.

```python
import jax
import jax.numpy as jnp
from jax import lax

D = 6144
FF = 24576
ROWS = 256
TOKENS = 1024
N_GX = 4
N_GY = 4
N_GZ = 16


def spiked(values, stream_key, source, target, parts, factor):
    owner, partner = [(jnp.arange(values.shape[axis_at]) // (values.shape[axis_at] // parts)).reshape([-1 if axis == axis_at else 1 for axis in range(values.ndim)]) for axis_at in (source, target)]
    chosen = jax.random.permutation(stream_key, parts)[partner]
    strong = (owner == chosen) | (owner == (partner + parts // 2) % parts)
    return jnp.where(strong, factor * values, values)


def block_levels(key, shape, split, low, high):
    gain = 1.0
    for axis_at, parts in split:
        steps = jax.random.uniform(jax.random.fold_in(jax.random.fold_in(key, 6), axis_at), (parts,), jnp.float32, low / len(split), high / len(split))
        gain = gain * jnp.repeat(jnp.exp(steps), shape[axis_at] // parts).reshape((-1,) + (1,) * (len(shape) - 1 - axis_at))
    return gain


def normal_values(rng, extent, scale, bound, cuts=(), dtype=jnp.bfloat16):
    result = scale * jax.random.normal(rng, extent, jnp.float32)
    if cuts:
        result = result * block_levels(rng, extent, cuts, -0.22, 0.18)
    return jnp.clip(result, -bound, bound).astype(dtype)


def noise_with(stream_key, extent, spread, limit, shards, heavy, dtype=jnp.bfloat16):
    values = spread * jax.random.normal(stream_key, extent, jnp.float32)
    if shards:
        values = values * block_levels(stream_key, extent, shards, -0.22, 0.18)
    return jnp.clip(spiked(values, jax.random.fold_in(stream_key, 3), *heavy), -limit, limit).astype(dtype)


def setup_inputs(seed: int = 0) -> dict:
    keys = jax.random.split(jax.random.key(seed), 7)
    tokens = normal_values(keys[0], (TOKENS, D), 1.0, 6.0, ((0, 16), (1, 16)))
    w_up = noise_with(keys[1], (D, FF), D ** -0.5, 0.109375, ((0, 16), (1, 16)), (0, 1, 16, 2.0))
    b_up = normal_values(keys[2], (FF,), 0.5, 3.0, ((0, 64),), jnp.float32)
    w_down = noise_with(keys[3], (FF, D), FF ** -0.5, 0.0546875, ((0, 16), (1, 16)), (1, 0, 16, 2.0))
    b_down = normal_values(keys[4], (D,), 0.5, 3.0, ((0, 16),), jnp.float32)
    cotangent = normal_values(keys[5], (TOKENS, D), 0.25, 1.5, ((0, 16), (1, 16)))
    return {"tokens": tokens, "w_up": w_up, "b_up": b_up, "w_down": w_down, "b_down": b_down, "cotangent": cotangent}


gelu_scale = 0.7978845608028654
gelu_cubic = 0.044715


def gelu_value(values):
    inner = gelu_scale * (values + gelu_cubic * values * values * values)
    return 0.5 * values * (1.0 + jnp.tanh(inner))


def gelu_slope(values):
    slope_tanh = jnp.tanh(gelu_scale * (values + gelu_cubic * values * values * values))
    return 0.5 * (1.0 + slope_tanh) + 0.5 * values * (1.0 - slope_tanh * slope_tanh) * gelu_scale * (1.0 + 3.0 * gelu_cubic * values * values)


def blocked_product(left, right):
    width = left.shape[1] // N_GZ

    def add_block(index, total):
        offset = (index * width).astype(jnp.int32)
        lhs = lax.dynamic_slice_in_dim(left, offset, width, 1)
        rhs = lax.dynamic_slice_in_dim(right, offset, width, 0)
        term = jnp.dot(lhs, rhs, preferred_element_type=jnp.float32)
        return total + lax.optimization_barrier(term.astype(jnp.bfloat16)).astype(jnp.float32)

    start_total = jnp.zeros((left.shape[0], right.shape[1]), jnp.float32)
    return lax.fori_loop(jnp.int32(0), jnp.int32(N_GZ), add_block, start_total)


def grouped_product(left, right):
    block_rows = ROWS // N_GX
    left_groups = left.reshape(N_GX, N_GY, block_rows, left.shape[1])
    right_groups = right.reshape(N_GX, N_GY, block_rows, right.shape[1])
    total = jnp.zeros((left.shape[1], right.shape[1]), jnp.float32)
    for group in range(N_GY):
        lhs = left_groups[:, group].reshape(N_GX * block_rows, left.shape[1])
        rhs = right_groups[:, group].reshape(N_GX * block_rows, right.shape[1])
        term = jnp.dot(lhs.T, rhs, preferred_element_type=jnp.float32)
        total = total + lax.optimization_barrier(term.astype(jnp.bfloat16)).astype(jnp.float32)
    return total


def reference(tokens, w_up, b_up, w_down, b_down, cotangent):
    pre_act = blocked_product(tokens, w_up) + b_up[None, :]
    act_full = gelu_value(pre_act).astype(jnp.bfloat16)
    output = (jnp.dot(act_full, w_down, preferred_element_type=jnp.float32) + b_down[None, :]).astype(jnp.bfloat16)
    grad_act = blocked_product(cotangent, w_down.T)
    grad_pre = (grad_act * gelu_slope(pre_act)).astype(jnp.bfloat16)
    grad_tokens = jnp.dot(grad_pre, w_up.T, preferred_element_type=jnp.float32).astype(jnp.bfloat16)
    grad_w_up = grouped_product(tokens, grad_pre).astype(jnp.bfloat16)
    grad_w_down = grouped_product(act_full, cotangent).astype(jnp.bfloat16)
    grad_b_up = jnp.sum(grad_pre.astype(jnp.float32), axis=0)
    grad_b_down = jnp.sum(cotangent.astype(jnp.float32), axis=0)
    return (output, grad_tokens, grad_w_up, grad_b_up, grad_w_down, grad_b_down)
```

```python
import jax
import jax.numpy as jnp
from jax import lax
from jax.sharding import PartitionSpec as P

gelu_scale = 0.7978845608028654
gelu_cubic = 0.044715


def gelu_both(v):
    t = jnp.tanh(gelu_scale * (v + gelu_cubic * v * v * v))
    value = 0.5 * v * (1.0 + t)
    slope = 0.5 * (1.0 + t) + 0.5 * v * (1.0 - t * t) * gelu_scale * (
        1.0 + 3.0 * gelu_cubic * v * v
    )
    return value, slope


def contract_rows(left, right):
    return lax.dot_general(
        left, right, (((0,), (0,)), ((), ())), preferred_element_type=jnp.float32
    )


def contract_cols(left, right):
    return lax.dot_general(
        left, right, (((1,), (1,)), ((), ())), preferred_element_type=jnp.float32
    )


def per_device(tokens, w_up, b_up, w_down, b_down, cotangent):
    rows_axes = ("gx", "gy")
    tok, cot = lax.all_gather((tokens, cotangent), rows_axes, axis=0, tiled=True)
    width = w_up.shape[1]
    small = b_up.shape[0]
    bias = lax.all_gather(b_up, "gz", axis=0, tiled=True)
    bias = lax.dynamic_slice_in_dim(bias, lax.axis_index("gy") * width, width, 0)

    partial_pre = jnp.dot(tok, w_up, preferred_element_type=jnp.float32).astype(jnp.bfloat16)
    partial_grad = contract_cols(cot, w_down).astype(jnp.bfloat16)
    pre = lax.psum_scatter(partial_pre, "gz", scatter_dimension=0, tiled=True)
    grad_act = lax.psum_scatter(partial_grad, "gz", scatter_dimension=0, tiled=True)
    value, slope = gelu_both(pre.astype(jnp.float32) + bias[None, :])
    act = lax.all_gather(value.astype(jnp.bfloat16), "gz", axis=0, tiled=True)
    grad_own = (grad_act.astype(jnp.float32) * slope).astype(jnp.bfloat16)
    grad = lax.all_gather(grad_own, "gz", axis=0, tiled=True)

    out = lax.psum_scatter(
        jnp.dot(act, w_down, preferred_element_type=jnp.float32).astype(jnp.bfloat16),
        rows_axes, scatter_dimension=0, tiled=True,
    )
    output = (out.astype(jnp.float32) + b_down[None, :]).astype(jnp.bfloat16)
    grad_w_down = contract_rows(act, cot).astype(jnp.bfloat16)
    grad_tokens = lax.psum_scatter(
        contract_cols(grad, w_up).astype(jnp.bfloat16), rows_axes, scatter_dimension=0, tiled=True
    )
    grad_w_up = contract_rows(tok, grad).astype(jnp.bfloat16)
    bias_sum = lax.all_gather(jnp.sum(grad.astype(jnp.float32), axis=0), "gy", axis=0, tiled=True)
    grad_b_up = lax.dynamic_slice_in_dim(bias_sum, lax.axis_index("gz") * small, small, 0)
    grad_b_down = jnp.sum(cot.astype(jnp.float32), axis=0)
    return (output, grad_tokens, grad_w_up, grad_b_up, grad_w_down, grad_b_down)


def solution(mesh):
    rows = P(("gx", "gy"), "gz")
    up = P("gz", ("gx", "gy"))
    down = P(("gx", "gy"), "gz")
    return jax.shard_map(
        per_device,
        mesh=mesh,
        in_specs=(rows, up, P(("gx", "gz")), down, P("gz"), rows),
        out_specs=(rows, rows, up, P(("gx", "gz")), down, P("gz")),
        check_vma=False,
    )
```

```python
import functools

import jax
import jax.numpy as jnp
from jax import lax
from jax.experimental import pallas as pl
from jax.experimental.pallas import tpu as pltpu
from jax.sharding import PartitionSpec as P

BF = jnp.bfloat16
F32 = jnp.float32
MESH = pl.DeviceIdType.MESH
gelu_scale = 0.7978845608028654
gelu_cubic = 0.044715
NC = 4
NZ = 8
TILE = 512
RS_GRAD, RS_PRE, AG_ACT, AG_GRAD = 0, 1, 2, 3
X_PRE, X_GRAD, X_AG, X_ACT = 0, 1, 2, 3


def gelu_both(v):
    t = jnp.tanh(gelu_scale * (v + gelu_cubic * v * v * v))
    value = 0.5 * v * (1.0 + t)
    slope = 0.5 * (1.0 + t) + 0.5 * v * (1.0 - t * t) * gelu_scale * (
        1.0 + 3.0 * gelu_cubic * v * v
    )
    return value, slope


def dot_nt(left, right):
    return lax.dot_general(left, right, (((1,), (1,)), ((), ())), preferred_element_type=F32)


def kernel(
    tok_ref, wup_ref, bup_ref, wdn_ref, bdn_ref, cot_ref,
    out_ref, gtok_ref, gwu_ref, gbu_ref, gwd_ref, gbd_ref,
    tc, tct, ppre, pgrad, xpre, zpre, zgrad, xgrad, act, grad, gact, acc_u, acc_d,
    opart, rcore, sx, rx, sy, ry, cs, bs, ball, brow,
    zs, zr, xs, xr, hs, hr, fs, fr, bzs, bzr,
):
    gx, gy, gz = lax.axis_index("gx"), lax.axis_index("gy"), lax.axis_index("gz")
    z, xl = lax.rem(gz, NZ), lax.div(gz, NZ)
    xo = 1 - xl
    xh, core = lax.div(gx, 2), lax.rem(gx, 2)
    feat, width = wup_ref.shape
    half = width // 2
    rows = tok_ref.shape[0]
    crow = 4 * rows
    unit = crow // 16

    def zi(j):
        return lax.rem(z + j + NZ, NZ)

    zdev = ({"gz": xl * NZ + zi(1)}, {"gz": xl * NZ + zi(-1)})
    xdev = {"gz": xo * NZ + z}
    coredev = {"gx": xh * 2 + 1 - core}
    xhdev = {"gx": (1 - xh) * 2 + core}

    def ydev(d):
        return {"gy": lax.rem(gy + d + 4, 4)}

    sign = (1, -1)

    def rcopy(src, dst, ss, rs, dev):
        return pltpu.make_async_remote_copy(
            src_ref=src, dst_ref=dst, send_sem=ss, recv_sem=rs,
            device_id=dev, device_id_type=MESH,
        )

    def hcols(ref, d):
        cols = pl.ds(d * half, half)
        return ref.at[..., cols] if not isinstance(ref, tuple) else None

    def rs_unit(op, u, t):
        return pgrad.at[u, t] if op == RS_GRAD else ppre.at[u, t, xl]

    def rs_land(op, u, d, r):
        return (zgrad if op == RS_GRAD else zpre).at[u, d, r - 1]

    def rs_copy(op, u, r, d):
        src = rs_unit(op, u, zi(sign[d] * (5 - r)))
        dst = rs_land(op, u, d, r)
        if r == 1:
            src, dst = hcols(src, d), hcols(dst, d)
        k = op * 8 + d * 4 + r - 1
        return rcopy(src, dst, zs.at[u, k], zr.at[u, k], zdev[d])

    def rs_step(op, u, r):
        for d in range(2):
            rs_copy(op, u, r - 1, d).wait_recv()
            dst, got = rs_unit(op, u, zi(sign[d] * (5 - r))), rs_land(op, u, d, r - 1)
            if r == 2:
                dst, got = hcols(dst, d), hcols(got, d)
            dst[...] = (dst[...].astype(F32) + got[...].astype(F32)).astype(BF)
            rs_copy(op, u, r, d).start()

    def ag_unit(op, u, t):
        return grad.at[u, t] if op == AG_GRAD else act.at[u, t, xl]

    def ag_copy(op, u, r, d, arriving):
        t = zi(-sign[d] * (r if arriving else r - 1))
        ref = ag_unit(op, u, t)
        if r == 4:
            ref = hcols(ref, d)
        k = op * 8 + d * 4 + r - 1
        return rcopy(ref, ref, zs.at[u, k], zr.at[u, k], zdev[d])

    def act_x(u, j, arriving):
        ref = act.at[u, zi(j), xo if arriving else xl]
        return rcopy(ref, ref, xs.at[u, X_ACT + j], xr.at[u, X_ACT + j], xdev)

    def ag_step(op, u, r):
        for d in range(2):
            ag_copy(op, u, r - 1, d, True).wait_recv()
            ag_copy(op, u, r, d, False).start()
            if op == AG_ACT:
                act_x(u, (-sign[d] * (r - 1)) % NZ, False).start()

    def x_pre(u):
        return rcopy(ppre.at[u, :, xo], xpre.at[u], xs.at[u, X_PRE], xr.at[u, X_PRE], xdev)

    def x_grad(u):
        return rcopy(pgrad.at[u, z, xo], xgrad.at[u], xs.at[u, X_GRAD], xr.at[u, X_GRAD], xdev)

    def x_ag(u, arriving):
        ref = grad.at[u, z, xo if arriving else xl]
        return rcopy(ref, ref, xs.at[u, X_AG], xr.at[u, X_AG], xdev)

    def bias_x(arriving):
        ref = ball.at[z, xo if arriving else xl]
        return rcopy(ref, ref, bzs.at[0], bzr.at[0], xdev)

    def bias_copy(r, d, arriving):
        ref = ball.at[zi(-sign[d] * (r if arriving else r - 1))]
        k = d * 4 + r
        return rcopy(ref, ref, bzs.at[k], bzr.at[k], zdev[d])

    def h_copy(k, src, dst, dev):
        return rcopy(src, dst, hs.at[k], hr.at[k], dev)

    own = tc.at[:, 0, xh, core]
    from_xh = tc.at[:, 0, 1 - xh, core]

    def h_xh():
        return h_copy(0, own, own, xhdev)

    def h_core():
        return h_copy(1, own, own, coredev)

    def h_core_fwd():
        return h_copy(2, from_xh, from_xh, coredev)

    def h_y(d):
        return h_copy(2 + d, own, tc.at[:, d, xh, core], ydev(-d))

    def h_y_fwd(d):
        return h_copy(5 + d, from_xh, tc.at[:, d, 1 - xh, core], ydev(-d))

    def h_core_y(d):
        ref = tc.at[:, d, :, core]
        return h_copy(8 + d, ref, ref, coredev)

    def part_pre(u):
        x = tc[0, u].reshape(crow, feat)

        @pl.loop(0, width // TILE)
        def _(j):
            cols = pl.ds(pl.multiple_of(j * TILE, TILE), TILE)
            v = jnp.dot(x, wup_ref[:, cols], preferred_element_type=F32)
            ppre[u, :, :, :, cols] = v.astype(BF).reshape(NZ, 2, unit, TILE)

    def part_grad(u):
        x = tc[1, u].reshape(crow, feat)

        @pl.loop(0, width // TILE)
        def _(j):
            cols = pl.ds(pl.multiple_of(j * TILE, TILE), TILE)
            v = dot_nt(x, wdn_ref[cols, :])
            pgrad[u, :, :, :, cols] = v.astype(BF).reshape(NZ, 2, unit, TILE)

    def transposed(u):
        tct[0, u] = tc[0, u].reshape(crow, feat).T
        tct[1, u] = tc[1, u].reshape(crow, feat).T

    def gelu_unit(u):
        v = (
            ppre[u, z, xl].astype(F32) + zpre[u, 0, 3].astype(F32) + zpre[u, 1, 3].astype(F32)
        ) + brow[0:1, :]
        value, slope = gelu_both(v)
        act[u, z, xl] = value.astype(BF)
        g = gact[u] + xgrad[u].astype(F32)
        grad[u, z, xl] = (g * slope).astype(BF)

    def f_core(u):
        return rcopy(opart.at[u, :, :, 1 - core], rcore.at[u], fs.at[u, 0], fr.at[u, 0], coredev)

    def f_xh(u):
        return rcopy(sx.at[u], rx.at[u], fs.at[u, 1], fr.at[u, 1], xhdev)

    def f_y(u):
        return rcopy(sy.at[u], ry.at[u], fs.at[u, 2], fr.at[u, 2], ydev(u))

    def final_1(u):
        for j in range(NZ):
            act_x(u, j, True).wait_recv()
        o = jnp.dot(act[u].reshape(crow, width), wdn_ref[...], preferred_element_type=F32)
        opart[u, 0] = o.astype(BF).reshape(2, 2, rows, feat)
        o = dot_nt(grad[u].reshape(crow, width), wup_ref[...])
        opart[u, 1] = o.astype(BF).reshape(2, 2, rows, feat)
        f_core(u).start()

    def weight_grad(acc, side, full, u):
        @pl.loop(0, width // TILE)
        def _(j):
            cols = pl.ds(pl.multiple_of(j * TILE, TILE), TILE)
            acc[:, cols] += jnp.dot(
                tct[side, u], full[u, :, :, :, cols].reshape(crow, TILE),
                preferred_element_type=F32,
            )

    def final_2(u):
        f_core(u).wait_recv()
        mine = opart[u, :, 1 - xh, core].astype(F32) + rcore[u, :, 1 - xh].astype(F32)
        sx[u] = mine.astype(BF)
        f_xh(u).start()

    def final_3(u):
        f_xh(u).wait_recv()
        mine = (
            opart[u, :, xh, core].astype(F32) + rcore[u, :, xh].astype(F32) + rx[u].astype(F32)
        ).astype(BF)

        @pl.when(u == 0)
        def _():
            ry[0] = mine

        @pl.when(u > 0)
        def _():
            sy[u] = mine
            f_y(u).start()

    def col_sum(u):
        cs[...] += jnp.sum(grad[u].reshape(crow // 8, 8, width).astype(F32), axis=0)

    for side, ref in ((0, tok_ref), (1, cot_ref)):
        tc[side, 0, xh, core] = ref[...]
    ball[z, xl] = jnp.broadcast_to(bup_ref[...], ball.shape[2:])
    acc_u[...] = jnp.zeros_like(acc_u)
    acc_d[...] = jnp.zeros_like(acc_d)
    cs[...] = jnp.zeros_like(cs)

    barrier = pltpu.get_barrier_semaphore()
    peers = (zdev[0], zdev[1], xdev, coredev, xhdev, ydev(1), ydev(2), ydev(3))
    for dev in peers:
        pl.semaphore_signal(barrier, inc=1, device_id=dev, device_id_type=MESH)
    pl.semaphore_wait(barrier, len(peers))

    h_xh().start()
    h_core().start()
    for d in (1, 2, 3):
        h_y(d).start()
    bias_x(False).start()
    h_xh().wait_recv()
    h_core_fwd().start()
    for d in (1, 2, 3):
        h_y_fwd(d).start()
    h_core().wait_recv()
    h_core_fwd().wait_recv()
    part_grad(0)
    part_pre(0)
    for d in (1, 2, 3):
        h_y(d).wait_recv()
        h_y_fwd(d).wait_recv()
        h_core_y(d).start()
    transposed(0)

    def slot(s, carry):
        ug, up, ua, uf = s, s - 1, s - 2, s - 3
        on_g = s <= 3
        on_p = (s >= 1) & (s <= 4)
        on_a = (s >= 2) & (s <= 5)
        on_f = s >= 3

        @pl.when(on_g)
        def _():
            x_pre(ug).start()
            for d in range(2):
                rs_copy(RS_GRAD, ug, 1, d).start()

        @pl.when(on_p)
        def _():
            x_pre(up).wait_recv()
            ppre[up, :, xl] = (ppre[up, :, xl].astype(F32) + xpre[up].astype(F32)).astype(BF)
            for d in range(2):
                rs_copy(RS_PRE, up, 1, d).start()

        @pl.when(on_a)
        def _():
            x_ag(ua, True).wait_recv()
            for d in range(2):
                ag_copy(AG_GRAD, ua, 1, d, False).start()

        @pl.when(s == 0)
        def _():
            bias_x(True).wait_recv()
            for d in range(2):
                bias_copy(1, d, False).start()

        for r in (2, 3, 4):
            @pl.when(on_g)
            def _():
                rs_step(RS_GRAD, ug, r)

            @pl.when(on_p)
            def _():
                rs_step(RS_PRE, up, r)

            @pl.when(on_a)
            def _():
                ag_step(AG_ACT, ua, r)
                ag_step(AG_GRAD, ua, r)

            @pl.when(s == 0)
            def _():
                for d in range(2):
                    bias_copy(r - 1, d, True).wait_recv()
                    if r < 4 or d == 0:
                        bias_copy(r, d, False).start()

            if r == 2:
                @pl.when(s < 3)
                def _():
                    un = s + 1
                    h_wait = rcopy(
                        tc.at[:, un, :, 1 - core], tc.at[:, un, :, 1 - core],
                        hs.at[8 + un], hr.at[8 + un], coredev,
                    )
                    h_wait.wait_recv()
                    part_grad(un)

                @pl.when(on_f)
                def _():
                    final_1(uf)

            if r == 3:
                @pl.when(s < 3)
                def _():
                    part_pre(s + 1)
                    transposed(s + 1)

                @pl.when(on_f)
                def _():
                    weight_grad(acc_u, 0, grad, uf)
                    final_2(uf)

            if r == 4:
                @pl.when(on_f)
                def _():
                    weight_grad(acc_d, 1, act, uf)
                    col_sum(uf)
                    final_3(uf)

        @pl.when(on_a)
        def _():
            for d in range(2):
                ag_copy(AG_ACT, ua, 4, d, True).wait_recv()
            act_x(ua, 4, False).start()
            for d in range(2):
                ag_copy(AG_GRAD, ua, 4, d, True).wait_recv()

        @pl.when(on_g)
        def _():
            for d in range(2):
                rs_copy(RS_GRAD, ug, 4, d).wait_recv()

            def total(side):
                return (
                    pgrad[ug, z, side].astype(F32)
                    + zgrad[ug, 0, 3, side].astype(F32)
                    + zgrad[ug, 1, 3, side].astype(F32)
                )

            pgrad[ug, z, xo] = total(xo).astype(BF)
            x_grad(ug).start()
            gact[ug] = total(xl)

        @pl.when(s == 0)
        def _():
            bias_copy(4, 0, True).wait_recv()
            for j in range(4):
                piece = gy * 4 + j
                brow[:, j * feat:(j + 1) * feat] = ball[lax.rem(piece, NZ), lax.div(piece, NZ)]

        @pl.when(on_p)
        def _():
            for d in range(2):
                rs_copy(RS_PRE, up, 4, d).wait_recv()
            x_grad(up).wait_recv()
            gelu_unit(up)
            x_ag(up, False).start()
            for d in range(2):
                ag_copy(AG_ACT, up, 1, d, False).start()
            act_x(up, 0, False).start()

        return carry

    lax.fori_loop(0, NC + 3, slot, 0)

    piece = pl.ds(pl.multiple_of(lax.rem(gz, 4) * feat, 128), feat)
    bs[gy] = cs[:, piece]

    def b_y(d):
        return rcopy(bs.at[gy], bs.at[gy], hs.at[11 + d], hr.at[11 + d], ydev(d))

    for d in (1, 2, 3):
        b_y(d).start()

    gwu_ref[...] = acc_u[...].astype(BF)
    gwd_ref[...] = acc_d[...].astype(BF).T
    gbd_ref[...] = jnp.sum(
        tc[1].reshape(NC * crow, feat).astype(F32), axis=0, keepdims=True
    )
    for d in (1, 2, 3):
        src = lax.rem(gy - d + 4, 4)
        rcopy(bs.at[src], bs.at[src], hs.at[11 + d], hr.at[11 + d], ydev(d)).wait_recv()
    gbu_ref[...] = jnp.sum(bs[lax.div(gz, 4)], axis=0, keepdims=True)
    for d in (1, 2, 3):
        f_y(d).wait_recv()
    total = (ry[0].astype(F32) + ry[1].astype(F32)) + (ry[2].astype(F32) + ry[3].astype(F32))
    out_ref[...] = (total[0] + bdn_ref[...]).astype(BF)
    gtok_ref[...] = total[1].astype(BF)

    def drain(u, carry):
        for d in range(2):
            for r in range(1, 5):
                rs_copy(RS_GRAD, u, r, d).wait_send()
                rs_copy(RS_PRE, u, r, d).wait_send()
                ag_copy(AG_ACT, u, r, d, False).wait_send()
                ag_copy(AG_GRAD, u, r, d, False).wait_send()
        x_pre(u).wait_send()
        x_grad(u).wait_send()
        x_ag(u, False).wait_send()
        for j in range(NZ):
            act_x(u, j, False).wait_send()
        f_core(u).wait_send()
        f_xh(u).wait_send()

        @pl.when(u > 0)
        def _():
            f_y(u).wait_send()
        return carry

    lax.fori_loop(0, NC, drain, 0)
    h_xh().wait_send()
    h_core().wait_send()
    h_core_fwd().wait_send()
    for d in (1, 2, 3):
        h_y(d).wait_send()
        h_y_fwd(d).wait_send()
        h_core_y(d).wait_send()
        b_y(d).wait_send()
    bias_x(False).wait_send()
    for r in range(1, 5):
        for d in range(2):
            if r < 4 or d == 0:
                bias_copy(r, d, False).wait_send()


def per_device(tokens, w_up, b_up, w_down, b_down, cotangent):
    rows, feat = tokens.shape
    width = w_up.shape[1]
    crow = 4 * rows
    unit = crow // 16
    vmem = pl.BlockSpec(memory_space=pltpu.VMEM)
    full = (NC, NZ, 2, unit, width)
    dma = pltpu.SemaphoreType.DMA
    scratch = [
        pltpu.VMEM((2, NC, 2, 2, rows, feat), BF),
        pltpu.VMEM((2, NC, feat, crow), BF),
        pltpu.VMEM(full, BF),
        pltpu.VMEM(full, BF),
        pltpu.VMEM((NC, NZ, unit, width), BF),
        pltpu.VMEM((NC, 2, 4, unit, width), BF),
        pltpu.VMEM((NC, 2, 4, 2, unit, width), BF),
        pltpu.VMEM((NC, unit, width), BF),
        pltpu.VMEM(full, BF),
        pltpu.VMEM(full, BF),
        pltpu.VMEM((NC, unit, width), F32),
        pltpu.VMEM((feat, width), F32),
        pltpu.VMEM((feat, width), F32),
        pltpu.VMEM((NC, 2, 2, 2, rows, feat), BF),
        pltpu.VMEM((NC, 2, 2, rows, feat), BF),
        pltpu.VMEM((NC, 2, rows, feat), BF),
        pltpu.VMEM((NC, 2, rows, feat), BF),
        pltpu.VMEM((NC, 2, rows, feat), BF),
        pltpu.VMEM((NC, 2, rows, feat), BF),
        pltpu.VMEM((8, width), F32),
        pltpu.VMEM((4, 8, feat), F32),
        pltpu.VMEM((NZ, 2, 8, feat), F32),
        pltpu.VMEM((8, width), F32),
        dma((NC, 32)), dma((NC, 32)),
        dma((NC, 11)), dma((NC, 11)),
        dma((15,)), dma((15,)),
        dma((NC, 3)), dma((NC, 3)),
        dma((9,)), dma((9,)),
    ]
    out, gtok, gwu, gbu, gwd, gbd = pl.pallas_call(
        kernel,
        out_shape=(
            jax.ShapeDtypeStruct((rows, feat), BF),
            jax.ShapeDtypeStruct((rows, feat), BF),
            jax.ShapeDtypeStruct((feat, width), BF),
            jax.ShapeDtypeStruct((1, feat), F32),
            jax.ShapeDtypeStruct((width, feat), BF),
            jax.ShapeDtypeStruct((1, feat), F32),
        ),
        in_specs=[vmem] * 6,
        out_specs=(vmem,) * 6,
        scratch_shapes=scratch,
        compiler_params=pltpu.CompilerParams(
            collective_id=0, has_side_effects=True, vmem_limit_bytes=60 * 2**20
        ),
        name="mlp_block",
    )(tokens, w_up, b_up[None, :], w_down, b_down[None, :], cotangent)
    return out, gtok, gwu, gbu[0], gwd, gbd[0]


def solution(mesh):
    rows = P(("gx", "gy"), "gz")
    up = P("gz", ("gx", "gy"))
    down = P(("gx", "gy"), "gz")
    return jax.shard_map(
        per_device,
        mesh=mesh,
        in_specs=(rows, up, P(("gx", "gz")), down, P("gz"), rows),
        out_specs=(rows, rows, up, P(("gx", "gz")), down, P("gz")),
        check_vma=False,
    )
```

```python
import jax
import jax.numpy as jnp
from jax import lax
from jax.experimental import pallas as pl
from jax.experimental.pallas import tpu as pltpu
from jax.sharding import PartitionSpec as P

BF = jnp.bfloat16
F32 = jnp.float32
MESH = pl.DeviceIdType.MESH
gelu_scale = 0.7978845608028654
gelu_cubic = 0.044715
NZ = 8
CHUNKS = ((0, 0), (1, 0), (1, 1), (2, 0), (2, 1), (3, 0), (3, 1), (0, 1))
NC = len(CHUNKS)
SIGN = (1, -1)
PRE, GRAD = 0, 1
LAG = 30

RS_X = ((1, 1, 0, 1, 1, 1, 0, 1), (0, 0, 1, 0, 1, 1, 0, 0))
AG_X = ((1, 1, 0, 1, 0, 1, 1, 1), (1, 0, 0, 1, 1, 0, 1, 0))
ORDER = (
    ("H", 0, 0), ("PP", 0, 1), ("PP", 0, 0), ("HF", 1, 0), ("HX", 0, 0), ("B1", 0, 0),
    ("R2", 0, 1), ("PP", 1, 1), ("HF", 3, 0), ("PP", 1, 0), ("B2", 0, 0), ("PP", 7, 1),
    ("R3", 0, 1), ("HF", 5, 0), ("PP", 3, 1), ("R1", 0, 0), ("B3", 0, 0), ("R2", 1, 1),
    ("R2", 7, 1), ("HF", 2, 0), ("PP", 3, 0), ("R4", 0, 1), ("R2", 3, 1), ("R2", 0, 0),
    ("HF", 4, 0), ("B4", 0, 0), ("PP", 2, 1), ("R1", 1, 0), ("R3", 1, 1), ("PP", 2, 0),
    ("HF", 6, 0), ("R3", 7, 1), ("PP", 4, 1), ("R5", 0, 1), ("PP", 4, 0), ("R3", 3, 1),
    ("R3", 0, 0), ("B5", 0, 0), ("R1", 3, 0), ("R2", 1, 0), ("PP", 5, 1), ("R4", 1, 1),
    ("R2", 2, 0), ("PP", 5, 0), ("R4", 7, 1), ("PP", 6, 1), ("R4", 3, 1), ("R4", 0, 0),
    ("R1", 2, 1), ("R3", 1, 0), ("R2", 3, 0), ("PP", 6, 0), ("R5", 1, 1), ("PP", 7, 0),
    ("R3", 2, 0), ("R1", 4, 1), ("R5", 7, 1), ("R2", 6, 1), ("D", 0, 0), ("R5", 3, 1),
    ("E", 0, 0), ("R4", 1, 0), ("R2", 2, 1), ("R3", 3, 0), ("R2", 6, 0), ("R1", 4, 0),
    ("R4", 2, 0), ("R2", 4, 1), ("R3", 6, 1), ("A2", 0, 0), ("A2", 0, 1), ("R3", 2, 1),
    ("R1", 5, 1), ("R4", 3, 0), ("R3", 6, 0), ("R2", 4, 0), ("R5", 2, 0), ("R3", 4, 1),
    ("R4", 6, 1), ("R1", 5, 0), ("A3", 0, 0), ("A3", 0, 1), ("E", 1, 0), ("R4", 2, 1),
    ("R2", 5, 1), ("R4", 6, 0), ("R3", 4, 0), ("R4", 4, 1), ("R1", 7, 0), ("R5", 6, 1),
    ("E", 3, 0), ("A4", 0, 0), ("A4", 0, 1), ("R2", 5, 0), ("A2", 1, 0), ("R3", 5, 1),
    ("R5", 6, 0), ("E", 2, 0), ("R4", 4, 0), ("R2", 7, 0), ("A2", 3, 0), ("A2", 3, 1),
    ("A5", 0, 0), ("A5", 0, 1), ("A1", 1, 1), ("R3", 5, 0), ("A3", 1, 0), ("R4", 5, 1),
    ("E", 4, 0), ("R3", 7, 0), ("A3", 3, 0), ("A3", 3, 1), ("A2", 1, 1), ("R4", 5, 0),
    ("E", 6, 0), ("A4", 1, 0), ("A1", 2, 0), ("A1", 2, 1), ("A2", 4, 1), ("R4", 7, 0),
    ("A4", 3, 0), ("A4", 3, 1), ("A3", 1, 1), ("F1", 0, 0), ("A2", 6, 0), ("A2", 6, 1),
    ("A5", 1, 0), ("E", 5, 0), ("A1", 4, 0), ("A2", 2, 0), ("F2", 0, 0), ("A2", 2, 1),
    ("A3", 4, 1), ("E", 7, 0), ("A5", 3, 0), ("A5", 3, 1), ("A4", 1, 1), ("A3", 6, 0),
    ("A3", 6, 1), ("A2", 5, 0), ("A2", 4, 0), ("A3", 2, 0), ("A3", 2, 1), ("A4", 4, 1),
    ("A2", 7, 0), ("F1", 1, 0), ("A4", 6, 0), ("A4", 6, 1), ("A3", 5, 0), ("A1", 5, 1),
    ("C", 1, 0), ("W", 1, 0), ("A3", 4, 0), ("F2", 1, 0), ("F1", 3, 0), ("A5", 4, 1),
    ("A4", 2, 0), ("A4", 2, 1), ("A1", 7, 1), ("A3", 7, 0), ("A5", 6, 0), ("W", 1, 1),
    ("A5", 6, 1), ("A4", 5, 0), ("F2", 3, 0), ("A2", 5, 1), ("A4", 4, 0), ("F1", 2, 0),
    ("A2", 7, 1), ("C", 3, 0), ("A5", 5, 0), ("A4", 7, 0), ("W", 3, 0), ("A3", 5, 1),
    ("F2", 2, 0), ("F1", 4, 0), ("A3", 7, 1), ("A5", 7, 0), ("F1", 6, 0), ("A4", 5, 1),
    ("F2", 4, 0), ("W", 3, 1), ("A4", 7, 1), ("F2", 6, 0), ("F1", 5, 0), ("F1", 7, 0),
    ("C", 5, 0), ("F2", 5, 0), ("W", 5, 0), ("F2", 7, 0), ("FX", 0, 0), ("W", 5, 1),
    ("C", 7, 0), ("W", 7, 0), ("W", 7, 1), ("END", 0, 0),
)


def gelu_both(v):
    t = jnp.tanh(gelu_scale * (v + gelu_cubic * v * v * v))
    value = 0.5 * v * (1.0 + t)
    slope = 0.5 * (1.0 + t) + 0.5 * v * (1.0 - t * t) * gelu_scale * (
        1.0 + 3.0 * gelu_cubic * v * v
    )
    return value, slope


def dot_nn(left, right):
    return jnp.dot(left, right, preferred_element_type=F32)


def dot_nt(left, right):
    return lax.dot_general(left, right, (((1,), (1,)), ((), ())), preferred_element_type=F32)


def kernel(
    tok_ref, wup_ref, bup_ref, wdn_ref, bdn_ref, cot_ref,
    out_ref, gtok_ref, gwu_ref, gbu_ref, gwd_ref, gbd_ref,
    tc, tct, part, zland, xland, own, full, acc_u, acc_d,
    opart, rcore, sy, ry, sx, rx, cs, bs, ball, brow,
    rzs, rzr, azs, azr, rxs, rxr, axs, axr, hs, hr, fs, fr, bzs, bzr,
):
    gx, gy, gz = lax.axis_index("gx"), lax.axis_index("gy"), lax.axis_index("gz")
    z, xl = lax.rem(gz, NZ), lax.div(gz, NZ)
    xh, core = lax.div(gx, 2), lax.rem(gx, 2)
    feat, width = wup_ref.shape
    half = width // 2
    rows = tok_ref.shape[0]
    crow = 2 * rows
    unit = crow // NZ

    def zi(j):
        return lax.rem(z + j + NZ, NZ)

    def side(x, shift, size):
        return pl.ds(pl.multiple_of(x * half + shift, 128), size)

    mine, theirs = side(xl, 0, half), side(1 - xl, 0, half)
    zdev = ({"gz": xl * NZ + zi(1)}, {"gz": xl * NZ + zi(-1)})
    xdev = {"gz": (1 - xl) * NZ + z}
    coredev = {"gx": xh * 2 + 1 - core}
    xhdev = {"gx": (1 - xh) * 2 + core}

    def ydev(d):
        return {"gy": lax.rem(gy + d + 4, 4)}

    def rcopy(src, dst, ss, rs, dev):
        return pltpu.make_async_remote_copy(
            src_ref=src, dst_ref=dst, send_sem=ss, recv_sem=rs,
            device_id=dev, device_id_type=MESH,
        )

    sent = []
    now = [0]

    def start(copy):
        copy.start()
        sent.append((now[0], copy))

    def rs_part(op, c, r, d):
        wide = half if RS_X[op][c] else width
        return (d * wide // 2, wide // 2) if r == 1 else (0, wide)

    def rs_unit(op, c, t, shift, size):
        cols = side(xl, shift, size) if RS_X[op][c] else pl.ds(shift, size)
        return part.at[op, c, t, :, cols]

    def rs_copy(op, c, r, d):
        shift, size = rs_part(op, c, r, d)
        return rcopy(
            rs_unit(op, c, zi(SIGN[d] * (5 - r)), shift, size),
            zland.at[op, c, d, r - 1, :, pl.ds(shift, size)],
            rzs.at[op, c, d * 4 + r - 1], rzr.at[op, c, d * 4 + r - 1], zdev[d],
        )

    def rs_step(op, c, r):
        for d in range(2):
            rs_copy(op, c, r - 1, d).wait_recv()
            shift, size = rs_part(op, c, r - 1, d)
            dst = rs_unit(op, c, zi(SIGN[d] * (5 - r)), shift, size)
            got = zland[op, c, d, r - 2, :, shift:shift + size]
            dst[...] = (dst[...].astype(F32) + got.astype(F32)).astype(BF)
            start(rs_copy(op, c, r, d))

    def rs_x(op, c):
        if RS_X[op][c]:
            src, dst = part.at[op, c, :, :, theirs], xland.at[op, c]
        else:
            src, dst = part.at[op, c, z, :, theirs], xland.at[op, c, 0]
        return rcopy(src, dst, rxs.at[op, c], rxr.at[op, c], xdev)

    def rs_total(op, c, cols, land):
        return (
            part[op, c, z, :, cols].astype(F32)
            + zland[op, c, 0, 3, :, land].astype(F32)
            + zland[op, c, 1, 3, :, land].astype(F32)
        )

    def ag_copy(op, c, r, d, arriving):
        t = zi(-SIGN[d] * (r if arriving else r - 1))
        wide = half if AG_X[op][c] else width
        shift, size = (d * wide // 2, wide // 2) if r == 4 else (0, wide)
        cols = side(xl, shift, size) if AG_X[op][c] else pl.ds(shift, size)
        ref = full.at[op, c, t, :, cols]
        k = d * 4 + r - 1
        return rcopy(ref, ref, azs.at[op, c, k], azr.at[op, c, k], zdev[d])

    def ag_x(op, c, j, arriving):
        ref = full.at[op, c, zi(j), :, theirs if arriving else mine]
        return rcopy(ref, ref, axs.at[op, c, j], axr.at[op, c, j], xdev)

    def bias_x(arriving):
        ref = ball.at[z, 1 - xl if arriving else xl]
        return rcopy(ref, ref, bzs.at[0], bzr.at[0], xdev)

    def bias_copy(r, d, arriving):
        ref = ball.at[zi(-SIGN[d] * (r if arriving else r - 1))]
        k = d * 4 + r
        return rcopy(ref, ref, bzs.at[k], bzr.at[k], zdev[d])

    chunk_of = {pair: c for c, pair in enumerate(CHUNKS)}
    own_rows = tc.at[:, 0, core]
    last = chunk_of[(0, 1)]
    other_rows = tc.at[:, last, core]

    def h_copy(k, src, dst, dev):
        return rcopy(src, dst, hs.at[k], hr.at[k], dev)

    def h_xh():
        return h_copy(0, own_rows, other_rows, xhdev)

    def h_y(c):
        u, h = CHUNKS[c]
        return h_copy(c, other_rows if h else own_rows, tc.at[:, c, core], ydev(-u))

    def h_core(c):
        ref = tc.at[:, c, core]
        return h_copy(NC + c, ref, ref, coredev)

    def f_core(c):
        return rcopy(opart.at[c, :, 1 - core], rcore.at[c], fs.at[0, c], fr.at[0, c], coredev)

    def f_y(c):
        return rcopy(sy.at[c], ry.at[c], fs.at[1, c], fr.at[1, c], ydev(CHUNKS[c][0]))

    def f_xh():
        return rcopy(sx, rx, fs.at[0, NC], fr.at[0, NC], xhdev)

    def ry_sum(h):
        picks = [c for c in range(NC) if CHUNKS[c][1] == h]
        for c in picks:
            if CHUNKS[c][0]:
                f_y(c).wait_recv()
        a, b, c, d = [ry[p].astype(F32) for p in picks]
        return (a + b) + (c + d)

    def b_y(d, arriving):
        ref = bs.at[lax.rem(gy - d + 4, 4) if arriving else gy]
        return rcopy(ref, ref, hs.at[2 * NC + d - 1], hr.at[2 * NC + d - 1], ydev(d))

    def ev_H(c, op):
        start(h_xh())
        start(h_core(0))
        for k in (1, 3, 5):
            start(h_y(k))
        start(bias_x(False))

    def ev_HX(c, op):
        h_xh().wait_recv()
        start(h_core(last))
        for k in (2, 4, 6):
            start(h_y(k))

    def ev_HF(c, op):
        h_y(c).wait_recv()
        start(h_core(c))

    arrived = set()

    def ev_PP(c, op):
        if c not in arrived:
            arrived.add(c)
            ref = tc.at[:, c, 1 - core]
            h_copy(NC + c, ref, ref, coredev).wait_recv()
        x = tc[op, c].reshape(crow, feat)

        @pl.loop(0, 2)
        def _(j):
            cols = pl.ds(pl.multiple_of(j * half, half), half)
            v = dot_nt(x, wdn_ref[cols, :]) if op == GRAD else dot_nn(x, wup_ref[:, cols])
            part[op, c, :, :, cols] = v.astype(BF).reshape(NZ, unit, half)

        if RS_X[op][c]:
            start(rs_x(op, c))
        else:
            for d in range(2):
                start(rs_copy(op, c, 1, d))

    def ev_R1(c, op):
        rs_x(op, c).wait_recv()
        part[op, c, :, :, mine] = (
            part[op, c, :, :, mine].astype(F32) + xland[op, c].astype(F32)
        ).astype(BF)
        for d in range(2):
            start(rs_copy(op, c, 1, d))

    def ev_R5(c, op):
        for d in range(2):
            rs_copy(op, c, 4, d).wait_recv()
        part[op, c, z, :, theirs] = rs_total(op, c, theirs, theirs).astype(BF)
        start(rs_x(op, c))
        own[op, c] = rs_total(op, c, mine, mine)

    def ev_E(c, op):
        got = []
        for o in (PRE, GRAD):
            if RS_X[o][c]:
                for d in range(2):
                    rs_copy(o, c, 4, d).wait_recv()
                got.append(rs_total(o, c, mine, pl.ds(0, half)))
            else:
                rs_x(o, c).wait_recv()
                got.append(own[o, c] + xland[o, c, 0].astype(F32))
        value, slope = gelu_both(got[PRE] + brow[0:1, :])
        full[PRE, c, z, :, mine] = value.astype(BF)
        full[GRAD, c, z, :, mine] = (got[GRAD] * slope).astype(BF)
        for o in (PRE, GRAD):
            if AG_X[o][c]:
                for d in range(2):
                    start(ag_copy(o, c, 1, d, False))
            start(ag_x(o, c, 0, False))

    def ev_A1(c, op):
        ag_x(op, c, 0, True).wait_recv()
        for d in range(2):
            start(ag_copy(op, c, 1, d, False))

    def ag_step(c, op, r):
        for d in range(2):
            ag_copy(op, c, r - 1, d, True).wait_recv()
            start(ag_copy(op, c, r, d, False))
            if AG_X[op][c]:
                start(ag_x(op, c, (-SIGN[d] * (r - 1)) % NZ, False))

    def ev_A5(c, op):
        for d in range(2):
            ag_copy(op, c, 4, d, True).wait_recv()
        start(ag_x(op, c, 4, False))

    def ev_F1(c, op):
        for o in (PRE, GRAD):
            if AG_X[o][c]:
                for j in range(NZ):
                    ag_x(o, c, j, True).wait_recv()
            else:
                for d in range(2):
                    ag_copy(o, c, 4, d, True).wait_recv()
        v = dot_nn(full[PRE, c].reshape(crow, width), wdn_ref[...])
        opart[c, 0] = v.astype(BF).reshape(2, rows, feat)
        v = dot_nt(full[GRAD, c].reshape(crow, width), wup_ref[...])
        opart[c, 1] = v.astype(BF).reshape(2, rows, feat)
        start(f_core(c))

    def ev_F2(c, op):
        f_core(c).wait_recv()
        v = (opart[c, :, core].astype(F32) + rcore[c].astype(F32)).astype(BF)
        if CHUNKS[c][0]:
            sy[c] = v
            start(f_y(c))
        else:
            ry[c] = v

    def ev_FX(c, op):
        sx[...] = ry_sum(1).astype(BF)
        start(f_xh())

    def ev_W(c, op):
        p = c // 2
        acc, out, other = ((acc_u, gwu_ref, GRAD), (acc_d, None, PRE))[op]
        tct[op, p] = tc[op, c - 1:c + 1].reshape(2 * crow, feat).T

        @pl.loop(0, 3)
        def _(j):
            cols = pl.ds(pl.multiple_of(j * 512, 512), 512)
            v = dot_nn(tct[op, p], full[other, c - 1:c + 1, :, :, cols].reshape(2 * crow, 512))
            if p:
                v += acc[:, cols]
            if c == NC - 1 and op == PRE:
                gwu_ref[:, cols] = v.astype(BF)
            else:
                acc[:, cols] = v

        if c == NC - 1 and op == GRAD:
            gwd_ref[...] = acc_d[...].astype(BF).T

    def ev_C(c, op):
        v = full[GRAD, c - 1:c + 1].reshape(2 * crow // 8, 8, width).astype(F32)
        v = jnp.sum(v, axis=0)
        if c > 1:
            v += cs[...]
        cs[...] = v
        if c == NC - 1:
            piece = pl.ds(pl.multiple_of(lax.rem(gz, 4) * feat, 128), feat)
            bs[gy] = cs[:, piece]
            for d in (1, 2, 3):
                start(b_y(d, False))

    def ev_D(c, op):
        gbd_ref[...] = jnp.sum(tc[1].reshape(NC * crow, feat).astype(F32), axis=0)

    def bias_step(r):
        if r == 1:
            bias_x(True).wait_recv()
        else:
            for d in range(2):
                if r < 5 or d == 0:
                    bias_copy(r - 1, d, True).wait_recv()
        if r < 5:
            for d in range(2):
                if r < 4 or d == 0:
                    start(bias_copy(r, d, False))
        else:
            for j in range(2):
                piece = gy * 4 + xl * 2 + j
                brow[:, j * feat:(j + 1) * feat] = ball[lax.rem(piece, NZ), lax.div(piece, NZ)]

    def ev_END(c, op):
        for d in (1, 2, 3):
            b_y(d, True).wait_recv()
        gbu_ref[...] = jnp.sum(bs[lax.div(gz, 4)], axis=0)
        total = ry_sum(0)
        f_xh().wait_recv()
        total += rx[...].astype(F32)
        out_ref[...] = (total[0] + bdn_ref[...][None, :]).astype(BF)
        gtok_ref[...] = total[1].astype(BF)

    events = {
        "H": ev_H, "HX": ev_HX, "HF": ev_HF, "PP": ev_PP, "R1": ev_R1, "R5": ev_R5,
        "E": ev_E, "A1": ev_A1, "A5": ev_A5, "F1": ev_F1, "F2": ev_F2, "FX": ev_FX,
        "W": ev_W, "C": ev_C, "D": ev_D, "END": ev_END,
    }

    for i, ref in enumerate((tok_ref, cot_ref)):
        tc[i, 0, core] = ref[...]
    ball[z, xl] = jnp.broadcast_to(bup_ref[...][None, :], ball.shape[2:])

    barrier = pltpu.get_barrier_semaphore()
    peers = (zdev[0], zdev[1], xdev, coredev, xhdev, ydev(1), ydev(2), ydev(3))
    for dev in peers:
        pl.semaphore_signal(barrier, inc=1, device_id=dev, device_id_type=MESH)
    pl.semaphore_wait(barrier, len(peers))

    for now[0], (kind, c, op) in enumerate(ORDER):
        if kind in ("R2", "R3", "R4"):
            rs_step(op, c, int(kind[1]))
        elif kind in ("A2", "A3", "A4"):
            ag_step(c, op, int(kind[1]))
        elif kind[0] == "B":
            bias_step(int(kind[1]))
        else:
            events[kind](c, op)
        while sent and sent[0][0] <= now[0] - LAG:
            sent.pop(0)[1].wait_send()
    for _, copy in sent:
        copy.wait_send()


def per_device(tokens, w_up, b_up, w_down, b_down, cotangent):
    rows, feat = tokens.shape
    width = w_up.shape[1]
    half = width // 2
    unit = 2 * rows // NZ
    vmem = pl.BlockSpec(memory_space=pltpu.VMEM)
    dma = pltpu.SemaphoreType.DMA
    scratch = [
        pltpu.VMEM((2, NC, 2, rows, feat), BF),
        pltpu.VMEM((2, NC // 2, feat, 4 * rows), BF),
        pltpu.VMEM((2, NC, NZ, unit, width), BF),
        pltpu.VMEM((2, NC, 2, 4, unit, width), BF),
        pltpu.VMEM((2, NC, NZ, unit, half), BF),
        pltpu.VMEM((2, NC, unit, half), F32),
        pltpu.VMEM((2, NC, NZ, unit, width), BF),
        pltpu.VMEM((feat, width), F32),
        pltpu.VMEM((feat, width), F32),
        pltpu.VMEM((NC, 2, 2, rows, feat), BF),
        pltpu.VMEM((NC, 2, rows, feat), BF),
        pltpu.VMEM((NC, 2, rows, feat), BF),
        pltpu.VMEM((NC, 2, rows, feat), BF),
        pltpu.VMEM((2, rows, feat), BF),
        pltpu.VMEM((2, rows, feat), BF),
        pltpu.VMEM((8, width), F32),
        pltpu.VMEM((4, 8, feat), F32),
        pltpu.VMEM((NZ, 2, 8, feat), F32),
        pltpu.VMEM((8, half), F32),
        dma((2, NC, 8)), dma((2, NC, 8)),
        dma((2, NC, 8)), dma((2, NC, 8)),
        dma((2, NC)), dma((2, NC)),
        dma((2, NC, NZ)), dma((2, NC, NZ)),
        dma((2 * NC + 3,)), dma((2 * NC + 3,)),
        dma((2, NC + 1)), dma((2, NC + 1)),
        dma((9,)), dma((9,)),
    ]
    return pl.pallas_call(
        kernel,
        out_shape=(
            jax.ShapeDtypeStruct((rows, feat), BF),
            jax.ShapeDtypeStruct((rows, feat), BF),
            jax.ShapeDtypeStruct((feat, width), BF),
            jax.ShapeDtypeStruct((feat,), F32),
            jax.ShapeDtypeStruct((width, feat), BF),
            jax.ShapeDtypeStruct((feat,), F32),
        ),
        in_specs=[vmem] * 6,
        out_specs=(vmem,) * 6,
        scratch_shapes=scratch,
        compiler_params=pltpu.CompilerParams(
            collective_id=0, has_side_effects=True, vmem_limit_bytes=60 * 2**20
        ),
        name="mlp_block",
    )(tokens, w_up, b_up, w_down, b_down, cotangent)


def solution(mesh):
    rows = P(("gx", "gy"), "gz")
    up = P("gz", ("gx", "gy"))
    down = P(("gx", "gy"), "gz")
    return jax.shard_map(
        per_device,
        mesh=mesh,
        in_specs=(rows, up, P(("gx", "gz")), down, P("gz"), rows),
        out_specs=(rows, rows, up, P(("gx", "gz")), down, P("gz")),
        check_vma=False,
    )
```

```python
import jax
import jax.numpy as jnp
from jax import lax
from jax.experimental import pallas as pl
from jax.experimental.pallas import tpu as pltpu
from jax.sharding import PartitionSpec as P

BF = jnp.bfloat16
F32 = jnp.float32
MESH = pl.DeviceIdType.MESH
gelu_scale = 0.7978845608028654
gelu_cubic = 0.044715
NZ = 8
CHUNKS = ((0, 0), (1, 0), (1, 1), (2, 0), (2, 1), (3, 0), (3, 1), (0, 1))
NC = len(CHUNKS)
SIGN = (1, -1)
PRE, GRAD = 0, 1
Z_POOL, X_POOL, POOL = 64, 64, 32

RS_X = ((1, 1, 0, 1, 1, 1, 0, 1), (0, 0, 1, 0, 1, 1, 0, 0))
AG_X = ((1, 1, 0, 1, 0, 1, 1, 1), (1, 0, 0, 1, 1, 0, 1, 0))
ORDER = (
    ("H", 0, 0), ("PP", 0, 1), ("PP", 0, 0), ("HF", 1, 0), ("HX", 0, 0), ("B1", 0, 0),
    ("R2", 0, 1), ("PP", 1, 1), ("HF", 3, 0), ("PP", 1, 0), ("B2", 0, 0), ("PP", 7, 1),
    ("R3", 0, 1), ("HF", 5, 0), ("PP", 3, 1), ("R1", 0, 0), ("B3", 0, 0), ("R2", 1, 1),
    ("R2", 7, 1), ("HF", 2, 0), ("PP", 3, 0), ("R4", 0, 1), ("R2", 3, 1), ("R2", 0, 0),
    ("HF", 4, 0), ("B4", 0, 0), ("PP", 2, 1), ("R1", 1, 0), ("R3", 1, 1), ("PP", 2, 0),
    ("HF", 6, 0), ("R3", 7, 1), ("PP", 4, 1), ("R5", 0, 1), ("PP", 4, 0), ("R3", 3, 1),
    ("R3", 0, 0), ("B5", 0, 0), ("R1", 3, 0), ("R2", 1, 0), ("PP", 5, 1), ("R4", 1, 1),
    ("R2", 2, 0), ("PP", 5, 0), ("R4", 7, 1), ("PP", 6, 1), ("R4", 3, 1), ("R4", 0, 0),
    ("R1", 2, 1), ("R3", 1, 0), ("R2", 3, 0), ("PP", 6, 0), ("R5", 1, 1), ("PP", 7, 0),
    ("R3", 2, 0), ("R1", 4, 1), ("R5", 7, 1), ("R2", 6, 1), ("D", 0, 0), ("R5", 3, 1),
    ("E", 0, 0), ("R4", 1, 0), ("R2", 2, 1), ("R3", 3, 0), ("R2", 6, 0), ("R1", 4, 0),
    ("R4", 2, 0), ("R2", 4, 1), ("R3", 6, 1), ("A2", 0, 0), ("A2", 0, 1), ("R3", 2, 1),
    ("R1", 5, 1), ("R4", 3, 0), ("R3", 6, 0), ("R2", 4, 0), ("R5", 2, 0), ("R3", 4, 1),
    ("R4", 6, 1), ("R1", 5, 0), ("A3", 0, 0), ("A3", 0, 1), ("E", 1, 0), ("R4", 2, 1),
    ("R2", 5, 1), ("R4", 6, 0), ("R3", 4, 0), ("R4", 4, 1), ("R1", 7, 0), ("R5", 6, 1),
    ("E", 3, 0), ("A4", 0, 0), ("A4", 0, 1), ("R2", 5, 0), ("A2", 1, 0), ("R3", 5, 1),
    ("R5", 6, 0), ("E", 2, 0), ("R4", 4, 0), ("R2", 7, 0), ("A2", 3, 0), ("A2", 3, 1),
    ("A5", 0, 0), ("A5", 0, 1), ("A1", 1, 1), ("R3", 5, 0), ("A3", 1, 0), ("R4", 5, 1),
    ("E", 4, 0), ("R3", 7, 0), ("A3", 3, 0), ("A3", 3, 1), ("A2", 1, 1), ("R4", 5, 0),
    ("E", 6, 0), ("A4", 1, 0), ("A1", 2, 0), ("A1", 2, 1), ("A2", 4, 1), ("R4", 7, 0),
    ("A4", 3, 0), ("A4", 3, 1), ("A3", 1, 1), ("F1", 0, 0), ("A2", 6, 0), ("A2", 6, 1),
    ("A5", 1, 0), ("E", 5, 0), ("A1", 4, 0), ("A2", 2, 0), ("F2", 0, 0), ("A2", 2, 1),
    ("A3", 4, 1), ("E", 7, 0), ("A5", 3, 0), ("A5", 3, 1), ("A4", 1, 1), ("A3", 6, 0),
    ("A3", 6, 1), ("A2", 5, 0), ("A2", 4, 0), ("A3", 2, 0), ("A3", 2, 1), ("A4", 4, 1),
    ("A2", 7, 0), ("F1", 1, 0), ("A4", 6, 0), ("A4", 6, 1), ("A3", 5, 0), ("A1", 5, 1),
    ("C", 1, 0), ("W", 1, 0), ("A3", 4, 0), ("F2", 1, 0), ("F1", 3, 0), ("A5", 4, 1),
    ("A4", 2, 0), ("A4", 2, 1), ("A1", 7, 1), ("A3", 7, 0), ("A5", 6, 0), ("W", 1, 1),
    ("A5", 6, 1), ("A4", 5, 0), ("F2", 3, 0), ("A2", 5, 1), ("A4", 4, 0), ("F1", 2, 0),
    ("A2", 7, 1), ("C", 3, 0), ("A5", 5, 0), ("A4", 7, 0), ("W", 3, 0), ("A3", 5, 1),
    ("F2", 2, 0), ("F1", 4, 0), ("A3", 7, 1), ("A5", 7, 0), ("F1", 6, 0), ("A4", 5, 1),
    ("F2", 4, 0), ("W", 3, 1), ("A4", 7, 1), ("F2", 6, 0), ("F1", 5, 0), ("F1", 7, 0),
    ("C", 5, 0), ("F2", 5, 0), ("W", 5, 0), ("F2", 7, 0), ("FX", 0, 0), ("W", 5, 1),
    ("C", 7, 0), ("W", 7, 0), ("W", 7, 1), ("END", 0, 0),
)


def gelu_both(v):
    t = jnp.tanh(gelu_scale * (v + gelu_cubic * v * v * v))
    value = 0.5 * v * (1.0 + t)
    slope = 0.5 * (1.0 + t) + 0.5 * v * (1.0 - t * t) * gelu_scale * (
        1.0 + 3.0 * gelu_cubic * v * v
    )
    return value, slope


def dot_nn(left, right):
    return jnp.dot(left, right, preferred_element_type=F32)


def dot_nt(left, right):
    return lax.dot_general(left, right, (((1,), (1,)), ((), ())), preferred_element_type=F32)


def kernel(
    tok_ref, wup_hbm, bup_ref, wdn_hbm, bdn_ref, cot_ref,
    out_ref, gtok_ref, gwu_hbm, gbu_ref, gwd_hbm, gbd_ref,
    tc, tct, part, zland, xland, own, full, acc_u, acc_d,
    opart, rcore, sy, ry, sx, rx, cs, bs, ball, brow,
    wup_vm, wdn_vm, gwu_vm, gwd_vm,
    rzr, azr, rxr, axr, hr, fr, bzr, zpool, xpool, pool, ls,
):
    gx, gy, gz = lax.axis_index("gx"), lax.axis_index("gy"), lax.axis_index("gz")
    z, xl = lax.rem(gz, NZ), lax.div(gz, NZ)
    xh, core = lax.div(gx, 2), lax.rem(gx, 2)
    feat, width = wup_vm.shape
    half = width // 2
    rows = tok_ref.shape[0]
    crow = 2 * rows
    unit = crow // NZ

    def zi(j):
        return lax.rem(z + j + NZ, NZ)

    def side(x, shift, size):
        return pl.ds(pl.multiple_of(x * half + shift, 128), size)

    mine, theirs = side(xl, 0, half), side(1 - xl, 0, half)
    zdev = ({"gz": xl * NZ + zi(1)}, {"gz": xl * NZ + zi(-1)})
    xdev = {"gz": (1 - xl) * NZ + z}
    coredev = {"gx": xh * 2 + 1 - core}
    xhdev = {"gx": (1 - xh) * 2 + core}

    def ydev(d):
        return {"gy": lax.rem(gy + d + 4, 4)}

    def rcopy(message, send_sem):
        src, dst, recv_sem, dev = message
        return pltpu.make_async_remote_copy(
            src_ref=src, dst_ref=dst, send_sem=send_sem, recv_sem=recv_sem,
            device_id=dev, device_id_type=MESH,
        )

    slots = {id(p): ([None] * p.shape[0], [0]) for p in (zpool, xpool, pool)}

    def start(message, sems):
        held, count = slots[id(sems)]
        k = count[0] % len(held)
        count[0] += 1
        if held[k] is not None:
            held[k].wait_send()
        held[k] = rcopy(message, sems.at[k])
        held[k].start()

    def arrive(message):
        rcopy(message, pool.at[0]).wait_recv()

    def arrive_all(like, sem):
        pltpu.make_async_copy(like, like, sem).wait()

    def rs_part(op, c, r, d):
        wide = half if RS_X[op][c] else width
        return (d * wide // 2, wide // 2) if r == 1 else (0, wide)

    def rs_unit(op, c, t, shift, size):
        cols = side(xl, shift, size) if RS_X[op][c] else pl.ds(shift, size)
        return part.at[op, c, t, :, cols]

    def rs_copy(op, c, r, d):
        shift, size = rs_part(op, c, r, d)
        return (
            rs_unit(op, c, zi(SIGN[d] * (5 - r)), shift, size),
            zland.at[op, c, d, r - 1, :, pl.ds(shift, size)],
            rzr.at[op, c, r - 1], zdev[d],
        )

    def rs_arrive(op, c, r):
        wide = half if RS_X[op][c] else width
        like = zland.at[op, c, :, r - 1, :, pl.ds(0, wide // 2 if r == 1 else wide)]
        arrive_all(like, rzr.at[op, c, r - 1])

    def rs_step(op, c, r):
        rs_arrive(op, c, r - 1)
        for d in range(2):
            shift, size = rs_part(op, c, r - 1, d)
            dst = rs_unit(op, c, zi(SIGN[d] * (5 - r)), shift, size)
            got = zland[op, c, d, r - 2, :, shift:shift + size]
            dst[...] = (dst[...].astype(F32) + got.astype(F32)).astype(BF)
            start(rs_copy(op, c, r, d), zpool)

    def rs_x(op, c):
        if RS_X[op][c]:
            src, dst = part.at[op, c, :, :, theirs], xland.at[op, c]
        else:
            src, dst = part.at[op, c, z, :, theirs], xland.at[op, c, 0]
        return src, dst, rxr.at[op, c], xdev

    def rs_total(op, c, cols, land):
        return (
            part[op, c, z, :, cols].astype(F32)
            + zland[op, c, 0, 3, :, land].astype(F32)
            + zland[op, c, 1, 3, :, land].astype(F32)
        )

    def ag_copy(op, c, r, d):
        t = zi(-SIGN[d] * (r - 1))
        wide = half if AG_X[op][c] else width
        shift, size = (d * wide // 2, wide // 2) if r == 4 else (0, wide)
        cols = side(xl, shift, size) if AG_X[op][c] else pl.ds(shift, size)
        ref = full.at[op, c, t, :, cols]
        return ref, ref, azr.at[op, c, r - 1], zdev[d]

    def ag_arrive(op, c, r):
        wide = half if AG_X[op][c] else width
        like = zland.at[op, c, :, 0, :, pl.ds(0, wide // 2 if r == 4 else wide)]
        arrive_all(like, azr.at[op, c, r - 1])

    def ag_x(op, c, j):
        ref = full.at[op, c, zi(j), :, mine]
        return ref, ref, axr.at[op, c], xdev

    def bias_x():
        return ball.at[z, xl], ball.at[z, xl], bzr.at[0], xdev

    def bias_copy(r, d):
        ref = ball.at[zi(-SIGN[d] * (r - 1))]
        return ref, ref, bzr.at[r], zdev[d]

    chunk_of = {pair: c for c, pair in enumerate(CHUNKS)}
    own_rows = tc.at[:, 0, core]
    last = chunk_of[(0, 1)]
    other_rows = tc.at[:, last, core]

    def h_copy(k, src, dst, dev):
        return src, dst, hr.at[k], dev

    def h_xh():
        return h_copy(0, own_rows, other_rows, xhdev)

    def h_y(c):
        u, h = CHUNKS[c]
        return h_copy(c, other_rows if h else own_rows, tc.at[:, c, core], ydev(-u))

    def h_core(c):
        ref = tc.at[:, c, core]
        return h_copy(NC + c, ref, ref, coredev)

    def f_core(c):
        return opart.at[c, :, 1 - core], rcore.at[c], fr.at[0, c], coredev

    def f_y(c):
        return sy.at[c], ry.at[c], fr.at[1, c], ydev(CHUNKS[c][0])

    def f_xh():
        return sx, rx, fr.at[0, NC], xhdev

    def ry_sum(h):
        picks = [c for c in range(NC) if CHUNKS[c][1] == h]
        for c in picks:
            if CHUNKS[c][0]:
                arrive(f_y(c))
        a, b, c, d = [ry[p].astype(F32) for p in picks]
        return (a + b) + (c + d)

    def b_y(d):
        return bs.at[gy], bs.at[gy], hr.at[2 * NC], ydev(d)

    def ev_H(c, op):
        start(h_core(0), pool)
        start(h_xh(), pool)
        for k in (1, 3, 5):
            start(h_y(k), pool)
        start(bias_x(), xpool)

    def ev_HX(c, op):
        arrive(h_xh())
        start(h_core(last), pool)
        for k in (2, 4, 6):
            start(h_y(k), pool)

    def ev_HF(c, op):
        arrive(h_y(c))
        start(h_core(c), pool)

    arrived = set()

    def ev_PP(c, op):
        if c not in arrived:
            arrived.add(c)
            arrive(h_core(c))
        if c == 0:
            local(0 if op == GRAD else 1).wait()
        x = tc[op, c].reshape(crow, feat)

        @pl.loop(0, 2)
        def _(j):
            cols = pl.ds(pl.multiple_of(j * half, half), half)
            v = dot_nt(x, wdn_vm[cols, :]) if op == GRAD else dot_nn(x, wup_vm[:, cols])
            part[op, c, :, :, cols] = v.astype(BF).reshape(NZ, unit, half)

        if RS_X[op][c]:
            start(rs_x(op, c), xpool)
        else:
            for d in range(2):
                start(rs_copy(op, c, 1, d), zpool)

    def ev_R1(c, op):
        arrive(rs_x(op, c))
        part[op, c, :, :, mine] = (
            part[op, c, :, :, mine].astype(F32) + xland[op, c].astype(F32)
        ).astype(BF)
        for d in range(2):
            start(rs_copy(op, c, 1, d), zpool)

    def ev_R5(c, op):
        rs_arrive(op, c, 4)
        part[op, c, z, :, theirs] = rs_total(op, c, theirs, theirs).astype(BF)
        start(rs_x(op, c), xpool)
        own[op, c] = rs_total(op, c, mine, mine)

    def ev_E(c, op):
        got = []
        for o in (PRE, GRAD):
            if RS_X[o][c]:
                rs_arrive(o, c, 4)
                got.append(rs_total(o, c, mine, pl.ds(0, half)))
            else:
                arrive(rs_x(o, c))
                got.append(own[o, c] + xland[o, c, 0].astype(F32))
        value, slope = gelu_both(got[PRE] + brow[0:1, :])
        full[PRE, c, z, :, mine] = value.astype(BF)
        full[GRAD, c, z, :, mine] = (got[GRAD] * slope).astype(BF)
        for o in (PRE, GRAD):
            if AG_X[o][c]:
                for d in range(2):
                    start(ag_copy(o, c, 1, d), zpool)
            start(ag_x(o, c, 0), xpool)

    def ev_A1(c, op):
        arrive(ag_x(op, c, 0))
        for d in range(2):
            start(ag_copy(op, c, 1, d), zpool)

    def ag_step(c, op, r):
        ag_arrive(op, c, r - 1)
        for d in range(2):
            start(ag_copy(op, c, r, d), zpool)
            if AG_X[op][c]:
                start(ag_x(op, c, (-SIGN[d] * (r - 1)) % NZ), xpool)

    def ev_A5(c, op):
        ag_arrive(op, c, 4)
        start(ag_x(op, c, 4), xpool)

    def ev_F1(c, op):
        for o in (PRE, GRAD):
            if AG_X[o][c]:
                arrive_all(xland.at[o, c], axr.at[o, c])
            else:
                ag_arrive(o, c, 4)
        v = dot_nn(full[PRE, c].reshape(crow, width), wdn_vm[...])
        opart[c, 0] = v.astype(BF).reshape(2, rows, feat)
        v = dot_nt(full[GRAD, c].reshape(crow, width), wup_vm[...])
        opart[c, 1] = v.astype(BF).reshape(2, rows, feat)
        start(f_core(c), pool)

    def ev_F2(c, op):
        arrive(f_core(c))
        v = (opart[c, :, core].astype(F32) + rcore[c].astype(F32)).astype(BF)
        if CHUNKS[c][0]:
            sy[c] = v
            start(f_y(c), pool)
        else:
            ry[c] = v

    def ev_FX(c, op):
        sx[...] = ry_sum(1).astype(BF)
        start(f_xh(), pool)

    def ev_W(c, op):
        p = c // 2
        acc, out, other = ((acc_u, gwu_vm, GRAD), (acc_d, None, PRE))[op]
        tct[op, p] = tc[op, c - 1:c + 1].reshape(2 * crow, feat).T

        @pl.loop(0, 3)
        def _(j):
            cols = pl.ds(pl.multiple_of(j * 512, 512), 512)
            v = dot_nn(tct[op, p], full[other, c - 1:c + 1, :, :, cols].reshape(2 * crow, 512))
            if p:
                v += acc[:, cols]
            if c == NC - 1 and op == PRE:
                gwu_vm[:, cols] = v.astype(BF)
            else:
                acc[:, cols] = v

        if c == NC - 1 and op == PRE:
            local(2).start()
        if c == NC - 1 and op == GRAD:
            gwd_vm[...] = acc_d[...].astype(BF).T
            local(3).start()

    def ev_C(c, op):
        v = full[GRAD, c - 1:c + 1].reshape(2 * crow // 8, 8, width).astype(F32)
        v = jnp.sum(v, axis=0)
        if c > 1:
            v += cs[...]
        cs[...] = v
        if c == NC - 1:
            piece = pl.ds(pl.multiple_of(lax.rem(gz, 4) * feat, 128), feat)
            bs[gy] = cs[:, piece]
            for d in (1, 2, 3):
                start(b_y(d), pool)

    def ev_D(c, op):
        gbd_ref[...] = jnp.sum(tc[1].reshape(NC * crow, feat).astype(F32), axis=0)

    def bias_step(r):
        if r == 1:
            arrive(bias_x())
        else:
            arrive_all(ball.at[0:2 if r < 5 else 1], bzr.at[r - 1])
        if r < 5:
            for d in range(2 if r < 4 else 1):
                start(bias_copy(r, d), zpool)
        else:
            for j in range(2):
                piece = gy * 4 + xl * 2 + j
                brow[:, j * feat:(j + 1) * feat] = ball[lax.rem(piece, NZ), lax.div(piece, NZ)]

    def ev_END(c, op):
        arrive_all(bs.at[0:3], hr.at[2 * NC])
        gbu_ref[...] = jnp.sum(bs[lax.div(gz, 4)], axis=0)
        total = ry_sum(0)
        arrive(f_xh())
        total += rx[...].astype(F32)
        out_ref[...] = (total[0] + bdn_ref[...][None, :]).astype(BF)
        gtok_ref[...] = total[1].astype(BF)

    events = {
        "H": ev_H, "HX": ev_HX, "HF": ev_HF, "PP": ev_PP, "R1": ev_R1, "R5": ev_R5,
        "E": ev_E, "A1": ev_A1, "A5": ev_A5, "F1": ev_F1, "F2": ev_F2, "FX": ev_FX,
        "W": ev_W, "C": ev_C, "D": ev_D, "END": ev_END,
    }

    def local(k):
        src, dst = (
            (wdn_hbm, wdn_vm), (wup_hbm, wup_vm), (gwu_vm, gwu_hbm), (gwd_vm, gwd_hbm),
        )[k]
        return pltpu.make_async_copy(src, dst, ls.at[k])

    local(0).start()
    local(1).start()
    for i, ref in enumerate((tok_ref, cot_ref)):
        tc[i, 0, core] = ref[...]
    ball[z, xl] = jnp.broadcast_to(bup_ref[...][None, :], ball.shape[2:])

    barrier = pltpu.get_barrier_semaphore()
    peers = (zdev[0], zdev[1], xdev, coredev, xhdev, ydev(1), ydev(2), ydev(3))
    for dev in peers:
        pl.semaphore_signal(barrier, inc=1, device_id=dev, device_id_type=MESH)
    pl.semaphore_wait(barrier, len(peers))

    for kind, c, op in ORDER:
        if kind in ("R2", "R3", "R4"):
            rs_step(op, c, int(kind[1]))
        elif kind in ("A2", "A3", "A4"):
            ag_step(c, op, int(kind[1]))
        elif kind[0] == "B":
            bias_step(int(kind[1]))
        else:
            events[kind](c, op)
    for held, _ in slots.values():
        for copy in held:
            if copy is not None:
                copy.wait_send()
    local(2).wait()
    local(3).wait()


def hand_over(results):
    count = len(results)

    def move(*refs):
        source, target, held = refs[:count], refs[count:2 * count], refs[2 * count:3 * count]
        sems = refs[3 * count]
        first = [pltpu.make_async_copy(source[k], held[k], sems.at[0, k]) for k in range(count)]
        second = [pltpu.make_async_copy(held[k], target[k], sems.at[1, k]) for k in range(count)]
        for copy in first:
            copy.start()
        for k in range(count):
            first[k].wait()
            second[k].start()
        for copy in second:
            copy.wait()

    place = pl.BlockSpec(memory_space=pl.ANY)
    return pl.pallas_call(
        move,
        out_shape=tuple(jax.ShapeDtypeStruct(r.shape, r.dtype) for r in results),
        in_specs=[place] * count,
        out_specs=(place,) * count,
        scratch_shapes=[pltpu.VMEM(r.shape, r.dtype) for r in results]
        + [pltpu.SemaphoreType.DMA((2, count))],
        name="hand_over",
    )(*results)


def per_device(tokens, w_up, b_up, w_down, b_down, cotangent):
    rows, feat = tokens.shape
    width = w_up.shape[1]
    half = width // 2
    unit = 2 * rows // NZ
    vmem = pl.BlockSpec(memory_space=pltpu.VMEM)
    place = pl.BlockSpec(memory_space=pl.ANY)
    dma = pltpu.SemaphoreType.DMA
    scratch = [
        pltpu.VMEM((2, NC, 2, rows, feat), BF),
        pltpu.VMEM((2, NC // 2, feat, 4 * rows), BF),
        pltpu.VMEM((2, NC, NZ, unit, width), BF),
        pltpu.VMEM((2, NC, 2, 4, unit, width), BF),
        pltpu.VMEM((2, NC, NZ, unit, half), BF),
        pltpu.VMEM((2, NC, unit, half), F32),
        pltpu.VMEM((2, NC, NZ, unit, width), BF),
        pltpu.VMEM((feat, width), F32),
        pltpu.VMEM((feat, width), F32),
        pltpu.VMEM((NC, 2, 2, rows, feat), BF),
        pltpu.VMEM((NC, 2, rows, feat), BF),
        pltpu.VMEM((NC, 2, rows, feat), BF),
        pltpu.VMEM((NC, 2, rows, feat), BF),
        pltpu.VMEM((2, rows, feat), BF),
        pltpu.VMEM((2, rows, feat), BF),
        pltpu.VMEM((8, width), F32),
        pltpu.VMEM((4, 8, feat), F32),
        pltpu.VMEM((NZ, 2, 8, feat), F32),
        pltpu.VMEM((8, half), F32),
        pltpu.VMEM((feat, width), BF),
        pltpu.VMEM((width, feat), BF),
        pltpu.VMEM((feat, width), BF),
        pltpu.VMEM((width, feat), BF),
        dma((2, NC, 4)),
        dma((2, NC, 4)),
        dma((2, NC)),
        dma((2, NC)),
        dma((2 * NC + 1,)),
        dma((2, NC + 1)),
        dma((5,)),
        dma((Z_POOL,)),
        dma((X_POOL,)),
        dma((POOL,)),
        dma((4,)),
    ]
    results = pl.pallas_call(
        kernel,
        out_shape=(
            jax.ShapeDtypeStruct((rows, feat), BF),
            jax.ShapeDtypeStruct((rows, feat), BF),
            jax.ShapeDtypeStruct((feat, width), BF),
            jax.ShapeDtypeStruct((feat,), F32),
            jax.ShapeDtypeStruct((width, feat), BF),
            jax.ShapeDtypeStruct((feat,), F32),
        ),
        in_specs=[vmem, place, vmem, place, vmem, vmem],
        out_specs=(vmem, vmem, place, vmem, place, vmem),
        scratch_shapes=scratch,
        compiler_params=pltpu.CompilerParams(
            collective_id=0, has_side_effects=True, vmem_limit_bytes=60 * 2**20
        ),
        name="mlp_block",
    )(tokens, w_up, b_up, w_down, b_down, cotangent)
    return hand_over(results)


def solution(mesh):
    rows = P(("gx", "gy"), "gz")
    up = P("gz", ("gx", "gy"))
    down = P(("gx", "gy"), "gz")
    return jax.shard_map(
        per_device,
        mesh=mesh,
        in_specs=(rows, up, P(("gx", "gz")), down, P("gz"), rows),
        out_specs=(rows, rows, up, P(("gx", "gz")), down, P("gz")),
        check_vma=False,
    )
```

```python
import jax
import jax.numpy as jnp
from jax import lax
from jax.experimental import pallas as pl
from jax.experimental.pallas import tpu as pltpu
from jax.sharding import PartitionSpec as P

BF = jnp.bfloat16
F32 = jnp.float32
MESH = pl.DeviceIdType.MESH
gelu_scale = 0.7978845608028654
gelu_cubic = 0.044715
NZ = 8
CHUNKS = ((0, 0), (1, 0), (1, 1), (2, 0), (2, 1), (3, 0), (3, 1), (0, 1))
NC = len(CHUNKS)
SIGN = (1, -1)
PRE, GRAD = 0, 1
Z_POOL, X_POOL, POOL = 20, 20, 12

RS_X = ((1, 0, 1, 1, 0, 1, 0, 1), (0, 1, 0, 1, 1, 1, 0, 0))
AG_X = ((1, 0, 0, 1, 0, 0, 0, 0), (1, 1, 1, 1, 1, 1, 1, 1))
ORDER = (
    ("H", 0, 0), ("PP", 0, 1), ("PP", 0, 0), ("HX", 0, 0), ("HF", 1, 0), ("B1", 0, 0),
    ("R2", 0, 1), ("PP", 7, 1), ("HF", 3, 0), ("B2", 0, 0), ("PP", 1, 1), ("PP", 1, 0),
    ("R3", 0, 1), ("HF", 5, 0), ("PP", 3, 1), ("R1", 0, 0), ("B3", 0, 0), ("R2", 7, 1),
    ("HF", 2, 0), ("R2", 1, 0), ("PP", 3, 0), ("R4", 0, 1), ("R2", 0, 0), ("PP", 2, 1),
    ("HF", 4, 0), ("B4", 0, 0), ("PP", 2, 0), ("R1", 1, 1), ("R3", 1, 0), ("HF", 6, 0),
    ("R3", 7, 1), ("PP", 4, 1), ("R5", 0, 1), ("R3", 0, 0), ("R2", 2, 1), ("PP", 4, 0),
    ("R1", 3, 1), ("B5", 0, 0), ("R4", 1, 0), ("R2", 1, 1), ("PP", 5, 1), ("R4", 7, 1),
    ("R4", 0, 0), ("PP", 5, 0), ("R3", 2, 1), ("PP", 6, 1), ("R1", 3, 0), ("R2", 3, 1),
    ("R5", 1, 0), ("R2", 4, 0), ("R3", 1, 1), ("PP", 6, 0), ("R5", 7, 1), ("PP", 7, 0),
    ("D", 0, 0), ("R1", 2, 0), ("R4", 2, 1), ("R2", 3, 0), ("R3", 3, 1), ("R2", 6, 1),
    ("R3", 4, 0), ("R4", 1, 1), ("R2", 6, 0), ("R2", 2, 0), ("R1", 4, 1), ("R5", 2, 1),
    ("E", 0, 0), ("R4", 3, 1), ("R3", 3, 0), ("R3", 6, 1), ("R4", 4, 0), ("R1", 5, 1),
    ("R3", 6, 0), ("R3", 2, 0), ("R2", 4, 1), ("A2", 0, 0), ("A2", 0, 1), ("R4", 3, 0),
    ("R1", 5, 0), ("R4", 6, 1), ("E", 1, 0), ("R5", 4, 0), ("R2", 5, 1), ("R4", 6, 0),
    ("R4", 2, 0), ("R3", 4, 1), ("A3", 0, 0), ("A3", 0, 1), ("R1", 7, 0), ("E", 3, 0),
    ("R5", 6, 1), ("R2", 5, 0), ("A2", 1, 1), ("R3", 5, 1), ("R5", 6, 0), ("E", 2, 0),
    ("A1", 1, 0), ("R4", 4, 1), ("A4", 0, 0), ("A4", 0, 1), ("R2", 7, 0), ("A2", 3, 0),
    ("A2", 3, 1), ("R3", 5, 0), ("A3", 1, 1), ("R4", 5, 1), ("A2", 2, 1), ("A2", 1, 0),
    ("E", 6, 0), ("A1", 2, 0), ("A5", 0, 0), ("A5", 0, 1), ("R3", 7, 0), ("E", 4, 0),
    ("A3", 3, 0), ("A3", 3, 1), ("R4", 5, 0), ("A4", 1, 1), ("A3", 2, 1), ("A3", 1, 0),
    ("A2", 6, 1), ("A2", 2, 0), ("R4", 7, 0), ("A1", 6, 0), ("A2", 4, 1), ("A4", 3, 0),
    ("F1", 0, 0), ("F1", 0, 1), ("A1", 4, 0), ("A5", 1, 1), ("E", 5, 0), ("A4", 2, 1),
    ("A4", 1, 0), ("A4", 3, 1), ("F2", 0, 0), ("A3", 6, 1), ("F2", 0, 1), ("A3", 2, 0),
    ("E", 7, 0), ("A2", 6, 0), ("A3", 4, 1), ("A5", 3, 0), ("A2", 4, 0), ("A2", 5, 1),
    ("A5", 2, 1), ("F1", 1, 0), ("A5", 3, 1), ("W", 1, 1), ("A1", 5, 0), ("F1", 1, 1),
    ("A4", 2, 0), ("A2", 7, 1), ("A4", 6, 1), ("F2", 1, 0), ("C", 1, 0), ("A3", 6, 0),
    ("W", 1, 0), ("A4", 4, 1), ("F2", 1, 1), ("A3", 4, 0), ("A1", 7, 0), ("A3", 5, 1),
    ("A2", 5, 0), ("F1", 2, 0), ("F1", 3, 0), ("A5", 6, 1), ("A3", 7, 1), ("W", 3, 1),
    ("F1", 2, 1), ("F1", 3, 1), ("A5", 4, 1), ("A4", 4, 0), ("A4", 6, 0), ("F2", 2, 0),
    ("F2", 3, 0), ("A2", 7, 0), ("F2", 2, 1), ("C", 3, 0), ("A4", 5, 1), ("F2", 3, 1),
    ("W", 3, 0), ("A3", 5, 0), ("A4", 7, 1), ("F1", 4, 0), ("F1", 6, 1), ("F1", 6, 0),
    ("A3", 7, 0), ("A5", 5, 1), ("F2", 4, 0), ("F1", 4, 1), ("F2", 6, 1), ("A4", 5, 0),
    ("F2", 6, 0), ("A5", 7, 1), ("F2", 4, 1), ("A4", 7, 0), ("F1", 5, 1), ("F1", 5, 0),
    ("F1", 7, 1), ("C", 5, 0), ("F1", 7, 0), ("F2", 5, 1), ("F2", 5, 0), ("C", 7, 0),
    ("F2", 7, 1), ("FX", 0, 1), ("W", 5, 0), ("F2", 7, 0), ("FX", 0, 0), ("W", 5, 1),
    ("W", 7, 0), ("W", 7, 1), ("END", 0, 0),
)


def gelu_both(v):
    t = jnp.tanh(gelu_scale * (v + gelu_cubic * v * v * v))
    value = 0.5 * v * (1.0 + t)
    slope = 0.5 * (1.0 + t) + 0.5 * v * (1.0 - t * t) * gelu_scale * (
        1.0 + 3.0 * gelu_cubic * v * v
    )
    return value, slope


def dot_nn(left, right):
    return jnp.dot(left, right, preferred_element_type=F32)


def dot_nt(left, right):
    return lax.dot_general(left, right, (((1,), (1,)), ((), ())), preferred_element_type=F32)


def kernel(
    tok_hbm, wup_hbm, bup_hbm, wdn_hbm, bdn_hbm, cot_hbm,
    out_ref, gtok_ref, gwu_hbm, gbu_ref, gwd_hbm, gbd_ref,
    tc, tct, part, zland, xland, own, full, acc_u, acc_d,
    opart, rcore, sy, ry, sx, rx, cs, bs, ball, brow,
    wup_vm, wdn_vm, bup_vm, bdn_vm, gwu_vm, gwd_vm,
    zr, rxr, axr, hr, fr, bzr, zpool, xpool, pool, ls,
):
    gx, gy, gz = lax.axis_index("gx"), lax.axis_index("gy"), lax.axis_index("gz")
    z, xl = lax.rem(gz, NZ), lax.div(gz, NZ)
    xh, core = lax.div(gx, 2), lax.rem(gx, 2)
    feat, width = wup_vm.shape
    half = width // 2
    rows = tok_hbm.shape[0]
    crow = 2 * rows
    unit = crow // NZ

    def zi(j):
        return lax.rem(z + j + NZ, NZ)

    def side(x, shift, size):
        return pl.ds(pl.multiple_of(x * half + shift, 128), size)

    mine, theirs = side(xl, 0, half), side(1 - xl, 0, half)
    zdev = ({"gz": xl * NZ + zi(1)}, {"gz": xl * NZ + zi(-1)})
    xdev = {"gz": (1 - xl) * NZ + z}
    coredev = {"gx": xh * 2 + 1 - core}
    xhdev = {"gx": (1 - xh) * 2 + core}

    def ydev(d):
        return {"gy": lax.rem(gy + d + 4, 4)}

    def rcopy(message, send_sem):
        src, dst, recv_sem, dev = message
        return pltpu.make_async_remote_copy(
            src_ref=src, dst_ref=dst, send_sem=send_sem, recv_sem=recv_sem,
            device_id=dev, device_id_type=MESH,
        )

    slots = {id(p): ([None] * p.shape[0], [0]) for p in (zpool, xpool, pool)}

    def start(message, sems):
        held, count = slots[id(sems)]
        k = count[0] % len(held)
        count[0] += 1
        if held[k] is not None:
            held[k].wait_send()
        held[k] = rcopy(message, sems.at[k])
        held[k].start()

    def arrive(message):
        rcopy(message, pool.at[0]).wait_recv()

    def arrive_all(like, sem):
        pltpu.make_async_copy(like, like, sem).wait()

    def rs_part(op, c, r, d):
        wide = half if RS_X[op][c] else width
        return (d * wide // 2, wide // 2) if r == 1 else (0, wide)

    def rs_unit(op, c, t, shift, size):
        cols = side(xl, shift, size) if RS_X[op][c] else pl.ds(shift, size)
        return part.at[op, c, t, :, cols]

    def rs_copy(op, c, r, d):
        shift, size = rs_part(op, c, r, d)
        return (
            rs_unit(op, c, zi(SIGN[d] * (5 - r)), shift, size),
            zland.at[op, c, d, r - 1, :, pl.ds(shift, size)],
            zr.at[op, c, r % 2], zdev[d],
        )

    def rs_arrive(op, c, r):
        wide = half if RS_X[op][c] else width
        like = zland.at[op, c, :, r - 1, :, pl.ds(0, wide // 2 if r == 1 else wide)]
        arrive_all(like, zr.at[op, c, r % 2])

    def rs_step(op, c, r):
        rs_arrive(op, c, r - 1)
        for d in range(2):
            shift, size = rs_part(op, c, r - 1, d)
            dst = rs_unit(op, c, zi(SIGN[d] * (5 - r)), shift, size)
            got = zland[op, c, d, r - 2, :, shift:shift + size]
            dst[...] = (dst[...].astype(F32) + got.astype(F32)).astype(BF)
            start(rs_copy(op, c, r, d), zpool)

    def rs_x(op, c):
        if RS_X[op][c]:
            src, dst = part.at[op, c, :, :, theirs], xland.at[op, c]
        else:
            src, dst = part.at[op, c, z, :, theirs], xland.at[op, c, 0]
        return src, dst, rxr.at[op, c], xdev

    def rs_total(op, c, cols, land):
        return (
            part[op, c, z, :, cols].astype(F32)
            + zland[op, c, 0, 3, :, land].astype(F32)
            + zland[op, c, 1, 3, :, land].astype(F32)
        )

    def ag_copy(op, c, r, d):
        t = zi(-SIGN[d] * (r - 1))
        wide = half if AG_X[op][c] else width
        shift, size = (d * wide // 2, wide // 2) if r == 4 else (0, wide)
        cols = side(xl, shift, size) if AG_X[op][c] else pl.ds(shift, size)
        ref = full.at[op, c, t, :, cols]
        return ref, ref, zr.at[op, c, r % 2], zdev[d]

    def ag_arrive(op, c, r):
        wide = half if AG_X[op][c] else width
        like = zland.at[op, c, :, 0, :, pl.ds(0, wide // 2 if r == 4 else wide)]
        arrive_all(like, zr.at[op, c, r % 2])

    def ag_x(op, c, j):
        ref = full.at[op, c, zi(j), :, mine]
        return ref, ref, axr.at[op, c], xdev

    def bias_x():
        return ball.at[z, xl], ball.at[z, xl], bzr.at[0], xdev

    def bias_copy(r, d):
        ref = ball.at[zi(-SIGN[d] * (r - 1))]
        return ref, ref, bzr.at[r], zdev[d]

    chunk_of = {pair: c for c, pair in enumerate(CHUNKS)}
    own_rows = tc.at[:, 0, core]
    last = chunk_of[(0, 1)]
    other_rows = tc.at[:, last, core]

    def h_copy(k, src, dst, dev):
        return src, dst, hr.at[k], dev

    def h_xh():
        return h_copy(0, own_rows, other_rows, xhdev)

    def h_y(c):
        u, h = CHUNKS[c]
        return h_copy(c, other_rows if h else own_rows, tc.at[:, c, core], ydev(-u))

    def h_core(c):
        ref = tc.at[:, c, core]
        return h_copy(NC + c, ref, ref, coredev)

    def f_core(c, op):
        return opart.at[c, op, 1 - core], rcore.at[c, op], fr.at[0, op, c], coredev

    def f_y(c, op):
        return sy.at[c, op], ry.at[c, op], fr.at[1, op, c], ydev(CHUNKS[c][0])

    def f_xh(op):
        return sx.at[op], rx.at[op], fr.at[0, op, NC], xhdev

    def ry_sum(h, op):
        picks = [c for c in range(NC) if CHUNKS[c][1] == h]
        for c in picks:
            if CHUNKS[c][0]:
                arrive(f_y(c, op))
        a, b, c, d = [ry[p, op].astype(F32) for p in picks]
        return (a + b) + (c + d)

    def b_y(d):
        return bs.at[gy], bs.at[gy], hr.at[2 * NC], ydev(d)

    def ev_H(c, op):
        start(h_core(0), pool)
        start(h_xh(), pool)
        for k in (1, 3, 5):
            start(h_y(k), pool)
        start(bias_x(), xpool)

    def ev_HX(c, op):
        arrive(h_xh())
        start(h_core(last), pool)
        for k in (2, 4, 6):
            start(h_y(k), pool)

    def ev_HF(c, op):
        arrive(h_y(c))
        start(h_core(c), pool)

    arrived = set()

    def ev_PP(c, op):
        if c not in arrived:
            arrived.add(c)
            arrive(h_core(c))
        if c == 0:
            local(0 if op == GRAD else 1).wait()
        x = tc[op, c].reshape(crow, feat)

        @pl.loop(0, 2)
        def _(j):
            cols = pl.ds(pl.multiple_of(j * half, half), half)
            v = dot_nt(x, wdn_vm[cols, :]) if op == GRAD else dot_nn(x, wup_vm[:, cols])
            part[op, c, :, :, cols] = v.astype(BF).reshape(NZ, unit, half)

        if RS_X[op][c]:
            start(rs_x(op, c), xpool)
        else:
            for d in range(2):
                start(rs_copy(op, c, 1, d), zpool)

    def ev_R1(c, op):
        arrive(rs_x(op, c))
        part[op, c, :, :, mine] = (
            part[op, c, :, :, mine].astype(F32) + xland[op, c].astype(F32)
        ).astype(BF)
        for d in range(2):
            start(rs_copy(op, c, 1, d), zpool)

    def ev_R5(c, op):
        rs_arrive(op, c, 4)
        part[op, c, z, :, theirs] = rs_total(op, c, theirs, theirs).astype(BF)
        start(rs_x(op, c), xpool)
        own[op, c] = rs_total(op, c, mine, mine)

    def ev_E(c, op):
        got = []
        for o in (PRE, GRAD):
            if RS_X[o][c]:
                rs_arrive(o, c, 4)
                got.append(rs_total(o, c, mine, pl.ds(0, half)))
            else:
                arrive(rs_x(o, c))
                got.append(own[o, c] + xland[o, c, 0].astype(F32))
        value, slope = gelu_both(got[PRE] + brow[0:1, :])
        full[PRE, c, z, :, mine] = value.astype(BF)
        full[GRAD, c, z, :, mine] = (got[GRAD] * slope).astype(BF)
        for o in (PRE, GRAD):
            if AG_X[o][c]:
                for d in range(2):
                    start(ag_copy(o, c, 1, d), zpool)
            start(ag_x(o, c, 0), xpool)

    def ev_A1(c, op):
        arrive(ag_x(op, c, 0))
        for d in range(2):
            start(ag_copy(op, c, 1, d), zpool)

    def ag_step(c, op, r):
        ag_arrive(op, c, r - 1)
        for d in range(2):
            start(ag_copy(op, c, r, d), zpool)
            if AG_X[op][c]:
                start(ag_x(op, c, (-SIGN[d] * (r - 1)) % NZ), xpool)

    def ev_A5(c, op):
        ag_arrive(op, c, 4)
        start(ag_x(op, c, 4), xpool)

    def ev_F1(c, op):
        if AG_X[op][c]:
            arrive_all(xland.at[op, c], axr.at[op, c])
        else:
            ag_arrive(op, c, 4)
        left = full[op, c].reshape(crow, width)
        v = dot_nn(left, wdn_vm[...]) if op == PRE else dot_nt(left, wup_vm[...])
        opart[c, op] = v.astype(BF).reshape(2, rows, feat)
        start(f_core(c, op), pool)

    def ev_F2(c, op):
        arrive(f_core(c, op))
        v = (opart[c, op, core].astype(F32) + rcore[c, op].astype(F32)).astype(BF)
        if CHUNKS[c][0]:
            sy[c, op] = v
            start(f_y(c, op), pool)
        else:
            ry[c, op] = v

    def ev_FX(c, op):
        sx[op] = ry_sum(1, op).astype(BF)
        start(f_xh(op), pool)

    def ev_W(c, op):
        p = c // 2
        acc, out, other = ((acc_u, gwu_vm, GRAD), (acc_d, None, PRE))[op]
        tct[op, p] = tc[op, c - 1:c + 1].reshape(2 * crow, feat).T

        @pl.loop(0, 3)
        def _(j):
            cols = pl.ds(pl.multiple_of(j * 512, 512), 512)
            v = dot_nn(tct[op, p], full[other, c - 1:c + 1, :, :, cols].reshape(2 * crow, 512))
            if p:
                v += acc[:, cols]
            if c == NC - 1 and op == PRE:
                gwu_vm[:, cols] = v.astype(BF)
            else:
                acc[:, cols] = v

        if c == NC - 1 and op == PRE:
            local(2).start()
        if c == NC - 1 and op == GRAD:
            gwd_vm[...] = acc_d[...].astype(BF).T
            local(3).start()

    def ev_C(c, op):
        v = full[GRAD, c - 1:c + 1].reshape(2 * crow // 8, 8, width).astype(F32)
        v = jnp.sum(v, axis=0)
        if c > 1:
            v += cs[...]
        cs[...] = v
        if c == NC - 1:
            piece = pl.ds(pl.multiple_of(lax.rem(gz, 4) * feat, 128), feat)
            bs[gy] = cs[:, piece]
            for d in (1, 2, 3):
                start(b_y(d), pool)

    def ev_D(c, op):
        gbd_ref[...] = jnp.sum(tc[1].reshape(NC * crow, feat).astype(F32), axis=0)

    def bias_step(r):
        if r == 1:
            arrive(bias_x())
        else:
            arrive_all(ball.at[0:2 if r < 5 else 1], bzr.at[r - 1])
        if r < 5:
            for d in range(2 if r < 4 else 1):
                start(bias_copy(r, d), zpool)
        else:
            for j in range(2):
                piece = gy * 4 + xl * 2 + j
                brow[:, j * feat:(j + 1) * feat] = ball[lax.rem(piece, NZ), lax.div(piece, NZ)]

    def ev_END(c, op):
        arrive_all(bs.at[0:3], hr.at[2 * NC])
        gbu_ref[...] = jnp.sum(bs[lax.div(gz, 4)], axis=0)
        for o in (PRE, GRAD):
            total = ry_sum(0, o)
            arrive(f_xh(o))
            total += rx[o].astype(F32)
            if o == PRE:
                out_ref[...] = (total + bdn_vm[...][None, :]).astype(BF)
            else:
                gtok_ref[...] = total.astype(BF)

    events = {
        "H": ev_H, "HX": ev_HX, "HF": ev_HF, "PP": ev_PP, "R1": ev_R1, "R5": ev_R5,
        "E": ev_E, "A1": ev_A1, "A5": ev_A5, "F1": ev_F1, "F2": ev_F2, "FX": ev_FX,
        "W": ev_W, "C": ev_C, "D": ev_D, "END": ev_END,
    }

    def local(k):
        src, dst = (
            (wdn_hbm, wdn_vm), (wup_hbm, wup_vm), (gwu_vm, gwu_hbm), (gwd_vm, gwd_hbm),
            (tok_hbm, tc.at[0, 0, core]), (cot_hbm, tc.at[1, 0, core]),
            (bup_hbm, bup_vm), (bdn_hbm, bdn_vm),
        )[k]
        return pltpu.make_async_copy(src, dst, ls.at[k])

    for k in (4, 5, 6, 7, 0, 1):
        local(k).start()
    barrier = pltpu.get_barrier_semaphore()
    peers = (zdev[0], zdev[1], xdev, coredev, xhdev, ydev(1), ydev(2), ydev(3))
    for dev in peers:
        pl.semaphore_signal(barrier, inc=1, device_id=dev, device_id_type=MESH)
    for k in (4, 5, 6, 7):
        local(k).wait()
    ball[z, xl] = jnp.broadcast_to(bup_vm[...][None, :], ball.shape[2:])
    pl.semaphore_wait(barrier, len(peers))

    for kind, c, op in ORDER:
        if kind in ("R2", "R3", "R4"):
            rs_step(op, c, int(kind[1]))
        elif kind in ("A2", "A3", "A4"):
            ag_step(c, op, int(kind[1]))
        elif kind[0] == "B":
            bias_step(int(kind[1]))
        else:
            events[kind](c, op)
    for held, _ in slots.values():
        for copy in held:
            if copy is not None:
                copy.wait_send()
    local(2).wait()
    local(3).wait()


def hand_over(results):
    count = len(results)
    pieces = []
    for k, r in enumerate(results):
        parts = 4 if r.size > 2**18 else 1
        size = r.shape[0] // parts
        pieces += [(k, i * size, size) for i in range(parts)]

    def move(*refs):
        source, target, held = refs[:count], refs[count:2 * count], refs[2 * count:3 * count]
        sems = refs[3 * count]

        def copy(side, i):
            k, at, size = pieces[i]
            ends = (source[k], held[k], target[k])
            rows = pl.ds(at, size)
            return pltpu.make_async_copy(
                ends[side].at[rows], ends[side + 1].at[rows], sems.at[side, i]
            )

        for i in range(len(pieces)):
            copy(0, i).start()
        for i in range(len(pieces)):
            copy(0, i).wait()
            copy(1, i).start()
        for i in range(len(pieces)):
            copy(1, i).wait()

    place = pl.BlockSpec(memory_space=pl.ANY)
    return pl.pallas_call(
        move,
        out_shape=tuple(jax.ShapeDtypeStruct(r.shape, r.dtype) for r in results),
        in_specs=[place] * count,
        out_specs=(place,) * count,
        scratch_shapes=[pltpu.VMEM(r.shape, r.dtype) for r in results]
        + [pltpu.SemaphoreType.DMA((2, len(pieces)))],
        name="hand_over",
    )(*results)


def per_device(tokens, w_up, b_up, w_down, b_down, cotangent):
    rows, feat = tokens.shape
    width = w_up.shape[1]
    half = width // 2
    unit = 2 * rows // NZ
    vmem = pl.BlockSpec(memory_space=pltpu.VMEM)
    place = pl.BlockSpec(memory_space=pl.ANY)
    dma = pltpu.SemaphoreType.DMA
    scratch = [
        pltpu.VMEM((2, NC, 2, rows, feat), BF),
        pltpu.VMEM((2, NC // 2, feat, 4 * rows), BF),
        pltpu.VMEM((2, NC, NZ, unit, width), BF),
        pltpu.VMEM((2, NC, 2, 4, unit, width), BF),
        pltpu.VMEM((2, NC, NZ, unit, half), BF),
        pltpu.VMEM((2, NC, unit, half), F32),
        pltpu.VMEM((2, NC, NZ, unit, width), BF),
        pltpu.VMEM((feat, width), F32),
        pltpu.VMEM((feat, width), F32),
        pltpu.VMEM((NC, 2, 2, rows, feat), BF),
        pltpu.VMEM((NC, 2, rows, feat), BF),
        pltpu.VMEM((NC, 2, rows, feat), BF),
        pltpu.VMEM((NC, 2, rows, feat), BF),
        pltpu.VMEM((2, rows, feat), BF),
        pltpu.VMEM((2, rows, feat), BF),
        pltpu.VMEM((8, width), F32),
        pltpu.VMEM((4, 8, feat), F32),
        pltpu.VMEM((NZ, 2, 8, feat), F32),
        pltpu.VMEM((8, half), F32),
        pltpu.VMEM((feat, width), BF),
        pltpu.VMEM((width, feat), BF),
        pltpu.VMEM((feat,), F32),
        pltpu.VMEM((feat,), F32),
        pltpu.VMEM((feat, width), BF),
        pltpu.VMEM((width, feat), BF),
        dma((2, NC, 2)),
        dma((2, NC)),
        dma((2, NC)),
        dma((2 * NC + 1,)),
        dma((2, 2, NC + 1)),
        dma((5,)),
        dma((Z_POOL,)),
        dma((X_POOL,)),
        dma((POOL,)),
        dma((8,)),
    ]
    results = pl.pallas_call(
        kernel,
        out_shape=(
            jax.ShapeDtypeStruct((rows, feat), BF),
            jax.ShapeDtypeStruct((rows, feat), BF),
            jax.ShapeDtypeStruct((feat, width), BF),
            jax.ShapeDtypeStruct((feat,), F32),
            jax.ShapeDtypeStruct((width, feat), BF),
            jax.ShapeDtypeStruct((feat,), F32),
        ),
        in_specs=[place] * 6,
        out_specs=(vmem, vmem, place, vmem, place, vmem),
        scratch_shapes=scratch,
        compiler_params=pltpu.CompilerParams(
            collective_id=0, has_side_effects=True, vmem_limit_bytes=60 * 2**20
        ),
        name="mlp_block",
    )(tokens, w_up, b_up, w_down, b_down, cotangent)
    return hand_over(results)


def solution(mesh):
    rows = P(("gx", "gy"), "gz")
    up = P("gz", ("gx", "gy"))
    down = P(("gx", "gy"), "gz")
    return jax.shard_map(
        per_device,
        mesh=mesh,
        in_specs=(rows, up, P(("gx", "gz")), down, P("gz"), rows),
        out_specs=(rows, rows, up, P(("gx", "gz")), down, P("gz")),
        check_vma=False,
    )
```

```python
import jax
import jax.numpy as jnp
from jax import lax
from jax.experimental import pallas as pl
from jax.experimental.pallas import tpu as pltpu
from jax.sharding import PartitionSpec as P

BF = jnp.bfloat16
F32 = jnp.float32
MESH = pl.DeviceIdType.MESH
gelu_scale = 0.7978845608028654
gelu_cubic = 0.044715
NZ = 8
CHUNKS = ((0, 0), (1, 0), (1, 1), (2, 0), (2, 1), (3, 0), (3, 1), (0, 1))
NC = len(CHUNKS)
SIGN = (1, -1)
PRE, GRAD = 0, 1
Z_POOL, X_POOL, POOL = 20, 20, 12

RS_X = ((1, 1, 1, 0, 1, 1, 0, 1), (0, 0, 1, 0, 1, 0, 0, 1))
AG_X = ((1, 1, 1, 1, 0, 0, 1, 0), (1, 1, 0, 0, 1, 1, 0, 1))
ORDER = (
    ("H", 0, 0), ("PP", 0, 0), ("PP", 0, 1), ("HX", 0, 0), ("HF", 1, 0), ("B1", 0, 0),
    ("R2", 0, 1), ("PP", 7, 0), ("HF", 3, 0), ("PP", 1, 1), ("PP", 1, 0), ("B2", 0, 0),
    ("PP", 3, 0), ("R1", 0, 0), ("HF", 5, 0), ("R3", 0, 1), ("PP", 3, 1), ("HF", 2, 0),
    ("R2", 1, 1), ("B3", 0, 0), ("PP", 5, 1), ("R2", 3, 0), ("R2", 0, 0), ("HF", 4, 0),
    ("PP", 2, 0), ("R4", 0, 1), ("R2", 3, 1), ("R1", 7, 0), ("HF", 6, 0), ("R3", 1, 1),
    ("PP", 2, 1), ("B4", 0, 0), ("R2", 5, 1), ("PP", 4, 0), ("R3", 3, 0), ("R1", 1, 0),
    ("R3", 0, 0), ("PP", 4, 1), ("R5", 0, 1), ("PP", 5, 0), ("R3", 3, 1), ("R2", 7, 0),
    ("PP", 6, 0), ("B5", 0, 0), ("R4", 1, 1), ("R1", 2, 0), ("R3", 5, 1), ("PP", 7, 1),
    ("R4", 3, 0), ("R2", 1, 0), ("R4", 0, 0), ("PP", 6, 1), ("R4", 3, 1), ("D", 0, 0),
    ("R1", 2, 1), ("R2", 6, 0), ("R3", 7, 0), ("R5", 1, 1), ("R2", 2, 0), ("R4", 5, 1),
    ("R5", 3, 0), ("R1", 4, 0), ("R3", 1, 0), ("R2", 6, 1), ("R5", 3, 1), ("R2", 2, 1),
    ("R3", 6, 0), ("R4", 7, 0), ("R1", 4, 1), ("E", 0, 0), ("R3", 2, 0), ("R2", 4, 0),
    ("R5", 5, 1), ("R4", 1, 0), ("R3", 6, 1), ("R3", 2, 1), ("R4", 6, 0), ("R1", 5, 0),
    ("R2", 4, 1), ("A2", 0, 0), ("A2", 0, 1), ("R4", 2, 0), ("R3", 4, 0), ("R1", 7, 1),
    ("E", 1, 0), ("R4", 2, 1), ("E", 3, 0), ("R4", 6, 1), ("R3", 4, 1), ("A3", 0, 0),
    ("R2", 5, 0), ("A3", 0, 1), ("R5", 6, 0), ("R4", 4, 0), ("R2", 7, 1), ("A2", 1, 0),
    ("A2", 1, 1), ("E", 2, 0), ("A2", 3, 0), ("A1", 3, 1), ("R5", 6, 1), ("R4", 4, 1),
    ("A4", 0, 0), ("R3", 5, 0), ("A4", 0, 1), ("R3", 7, 1), ("A3", 1, 0), ("A3", 1, 1),
    ("A2", 2, 0), ("A3", 3, 0), ("A1", 2, 1), ("A2", 3, 1), ("E", 4, 0), ("A5", 0, 0),
    ("E", 6, 0), ("R4", 7, 1), ("A5", 0, 1), ("R4", 5, 0), ("A4", 1, 0), ("A4", 1, 1),
    ("A3", 2, 0), ("A4", 3, 0), ("A2", 2, 1), ("A3", 3, 1), ("A2", 4, 1), ("A2", 6, 0),
    ("A1", 4, 0), ("E", 7, 0), ("E", 5, 0), ("F1", 0, 0), ("A5", 1, 1), ("A5", 3, 0),
    ("A5", 1, 0), ("F1", 0, 1), ("A3", 2, 1), ("F2", 0, 0), ("A4", 2, 0), ("A1", 6, 1),
    ("A4", 3, 1), ("F2", 0, 1), ("A3", 4, 1), ("A3", 6, 0), ("A2", 4, 0), ("A2", 7, 1),
    ("A2", 5, 1), ("A4", 2, 1), ("A5", 2, 0), ("A1", 7, 0), ("A2", 6, 1), ("F1", 3, 1),
    ("A4", 4, 1), ("A1", 5, 0), ("A4", 6, 0), ("F1", 1, 1), ("C", 1, 0), ("A3", 4, 0),
    ("F1", 1, 0), ("A3", 7, 1), ("F1", 3, 0), ("F1", 2, 1), ("F2", 1, 0), ("C", 3, 0),
    ("A2", 7, 0), ("F2", 1, 1), ("F2", 3, 1), ("A3", 6, 1), ("F2", 2, 1), ("A5", 4, 1),
    ("F2", 3, 0), ("A3", 5, 1), ("W", 1, 1), ("A2", 5, 0), ("A5", 6, 0), ("W", 1, 0),
    ("A4", 4, 0), ("A4", 7, 1), ("F1", 2, 0), ("W", 3, 1), ("A3", 7, 0), ("W", 3, 0),
    ("A4", 5, 1), ("F2", 2, 0), ("A4", 6, 1), ("F1", 4, 1), ("A3", 5, 0), ("F1", 4, 0),
    ("A5", 7, 1), ("F1", 6, 0), ("F2", 4, 1), ("A4", 7, 0), ("A5", 5, 1), ("F2", 4, 0),
    ("F1", 6, 1), ("F2", 6, 0), ("A4", 5, 0), ("F1", 7, 1), ("F2", 6, 1), ("F1", 5, 1),
    ("C", 5, 0), ("F1", 7, 0), ("F2", 7, 1), ("C", 7, 0), ("F1", 5, 0), ("F2", 7, 0),
    ("FX", 0, 0), ("F2", 5, 1), ("W", 5, 0), ("FX", 0, 1), ("F2", 5, 0), ("W", 7, 0),
    ("W", 5, 1), ("W", 7, 1), ("END", 0, 0),
)


def gelu_both(v):
    t = jnp.tanh(gelu_scale * (v + gelu_cubic * v * v * v))
    value = 0.5 * v * (1.0 + t)
    slope = 0.5 * (1.0 + t) + 0.5 * v * (1.0 - t * t) * gelu_scale * (
        1.0 + 3.0 * gelu_cubic * v * v
    )
    return value, slope


def dot_nn(left, right):
    return jnp.dot(left, right, preferred_element_type=F32)


def dot_nt(left, right):
    return lax.dot_general(left, right, (((1,), (1,)), ((), ())), preferred_element_type=F32)


def kernel(
    tok_hbm, wup_hbm, bup_hbm, wdn_hbm, bdn_hbm, cot_hbm,
    out_hbm, gtok_hbm, gwu_hbm, gbu_hbm, gwd_hbm, gbd_hbm,
    tc, tct, part, zland, xland, own, full, acc_u, acc_d,
    opart, rcore, sy, ry, sx, rx, cs, bs, ball, brow,
    wup_vm, wdn_vm, bup_vm, bdn_vm, gwu_vm, gwd_vm,
    out_vm, gtok_vm, gbu_vm, gbd_vm,
    zr, rxr, axr, hr, fr, bzr, zpool, xpool, pool, ls,
):
    gx, gy, gz = lax.axis_index("gx"), lax.axis_index("gy"), lax.axis_index("gz")
    z, xl = lax.rem(gz, NZ), lax.div(gz, NZ)
    xh, core = lax.div(gx, 2), lax.rem(gx, 2)
    feat, width = wup_vm.shape
    half = width // 2
    rows = tok_hbm.shape[0]
    crow = 2 * rows
    unit = crow // NZ

    def zi(j):
        return lax.rem(z + j + NZ, NZ)

    def side(x, shift, size):
        return pl.ds(pl.multiple_of(x * half + shift, 128), size)

    mine, theirs = side(xl, 0, half), side(1 - xl, 0, half)
    zdev = ({"gz": xl * NZ + zi(1)}, {"gz": xl * NZ + zi(-1)})
    xdev = {"gz": (1 - xl) * NZ + z}
    coredev = {"gx": xh * 2 + 1 - core}
    xhdev = {"gx": (1 - xh) * 2 + core}

    def ydev(d):
        return {"gy": lax.rem(gy + d + 4, 4)}

    def rcopy(message, send_sem):
        src, dst, recv_sem, dev = message
        return pltpu.make_async_remote_copy(
            src_ref=src, dst_ref=dst, send_sem=send_sem, recv_sem=recv_sem,
            device_id=dev, device_id_type=MESH,
        )

    slots = {id(p): ([None] * p.shape[0], [0]) for p in (zpool, xpool, pool)}

    def start(message, sems):
        held, count = slots[id(sems)]
        k = count[0] % len(held)
        count[0] += 1
        if held[k] is not None:
            held[k].wait_send()
        held[k] = rcopy(message, sems.at[k])
        held[k].start()

    def arrive(message):
        rcopy(message, pool.at[0]).wait_recv()

    def arrive_all(like, sem):
        pltpu.make_async_copy(like, like, sem).wait()

    def rs_part(op, c, r, d):
        wide = half if RS_X[op][c] else width
        return (d * wide // 2, wide // 2) if r == 1 else (0, wide)

    def rs_unit(op, c, t, shift, size):
        cols = side(xl, shift, size) if RS_X[op][c] else pl.ds(shift, size)
        return part.at[op, c, t, :, cols]

    def rs_copy(op, c, r, d):
        shift, size = rs_part(op, c, r, d)
        return (
            rs_unit(op, c, zi(SIGN[d] * (5 - r)), shift, size),
            zland.at[op, c, d, r - 1, :, pl.ds(shift, size)],
            zr.at[op, c, r % 2], zdev[d],
        )

    def rs_arrive(op, c, r):
        wide = half if RS_X[op][c] else width
        like = zland.at[op, c, :, r - 1, :, pl.ds(0, wide // 2 if r == 1 else wide)]
        arrive_all(like, zr.at[op, c, r % 2])

    def rs_step(op, c, r):
        rs_arrive(op, c, r - 1)
        for d in range(2):
            shift, size = rs_part(op, c, r - 1, d)
            dst = rs_unit(op, c, zi(SIGN[d] * (5 - r)), shift, size)
            got = zland[op, c, d, r - 2, :, shift:shift + size]
            dst[...] = (dst[...].astype(F32) + got.astype(F32)).astype(BF)
            start(rs_copy(op, c, r, d), zpool)

    def rs_x(op, c):
        if RS_X[op][c]:
            src, dst = part.at[op, c, :, :, theirs], xland.at[op, c]
        else:
            src, dst = part.at[op, c, z, :, theirs], xland.at[op, c, 0]
        return src, dst, rxr.at[op, c], xdev

    def rs_total(op, c, cols, land):
        return (
            part[op, c, z, :, cols].astype(F32)
            + zland[op, c, 0, 3, :, land].astype(F32)
            + zland[op, c, 1, 3, :, land].astype(F32)
        )

    def ag_copy(op, c, r, d):
        t = zi(-SIGN[d] * (r - 1))
        wide = half if AG_X[op][c] else width
        shift, size = (d * wide // 2, wide // 2) if r == 4 else (0, wide)
        cols = side(xl, shift, size) if AG_X[op][c] else pl.ds(shift, size)
        ref = full.at[op, c, t, :, cols]
        return ref, ref, zr.at[op, c, r % 2], zdev[d]

    def ag_arrive(op, c, r):
        wide = half if AG_X[op][c] else width
        like = zland.at[op, c, :, 0, :, pl.ds(0, wide // 2 if r == 4 else wide)]
        arrive_all(like, zr.at[op, c, r % 2])

    def ag_x(op, c, j):
        ref = full.at[op, c, zi(j), :, mine]
        return ref, ref, axr.at[op, c], xdev

    def bias_x():
        return ball.at[z, xl], ball.at[z, xl], bzr.at[0], xdev

    def bias_copy(r, d):
        ref = ball.at[zi(-SIGN[d] * (r - 1))]
        return ref, ref, bzr.at[r], zdev[d]

    chunk_of = {pair: c for c, pair in enumerate(CHUNKS)}
    own_rows = tc.at[:, 0, core]
    last = chunk_of[(0, 1)]
    other_rows = tc.at[:, last, core]

    def h_copy(k, src, dst, dev):
        return src, dst, hr.at[k], dev

    def h_xh():
        return h_copy(0, own_rows, other_rows, xhdev)

    def h_y(c):
        u, h = CHUNKS[c]
        return h_copy(c, other_rows if h else own_rows, tc.at[:, c, core], ydev(-u))

    def h_core(c):
        ref = tc.at[:, c, core]
        return h_copy(NC + c, ref, ref, coredev)

    def f_core(c, op):
        return opart.at[c, op, 1 - core], rcore.at[c, op], fr.at[0, op, c], coredev

    def f_y(c, op):
        return sy.at[c, op], ry.at[c, op], fr.at[1, op, c], ydev(CHUNKS[c][0])

    def f_xh(op):
        return sx.at[op], rx.at[op], fr.at[0, op, NC], xhdev

    def ry_sum(h, op):
        picks = [c for c in range(NC) if CHUNKS[c][1] == h]
        for c in picks:
            if CHUNKS[c][0]:
                arrive(f_y(c, op))
        a, b, c, d = [ry[p, op].astype(F32) for p in picks]
        return (a + b) + (c + d)

    def b_y(d):
        return bs.at[gy], bs.at[gy], hr.at[2 * NC], ydev(d)

    def ev_H(c, op):
        start(h_core(0), pool)
        start(h_xh(), pool)
        for k in (1, 3, 5):
            start(h_y(k), pool)
        start(bias_x(), xpool)

    def ev_HX(c, op):
        arrive(h_xh())
        start(h_core(last), pool)
        for k in (2, 4, 6):
            start(h_y(k), pool)

    def ev_HF(c, op):
        arrive(h_y(c))
        start(h_core(c), pool)

    arrived = set()

    def ev_PP(c, op):
        if c not in arrived:
            arrived.add(c)
            arrive(h_core(c))
        if c == 0:
            local(0 if op == GRAD else 1).wait()
        x = tc[op, c].reshape(crow, feat)

        @pl.loop(0, 2)
        def _(j):
            cols = pl.ds(pl.multiple_of(j * half, half), half)
            v = dot_nt(x, wdn_vm[cols, :]) if op == GRAD else dot_nn(x, wup_vm[:, cols])
            part[op, c, :, :, cols] = v.astype(BF).reshape(NZ, unit, half)

        if RS_X[op][c]:
            start(rs_x(op, c), xpool)
        else:
            for d in range(2):
                start(rs_copy(op, c, 1, d), zpool)

    def ev_R1(c, op):
        arrive(rs_x(op, c))
        part[op, c, :, :, mine] = (
            part[op, c, :, :, mine].astype(F32) + xland[op, c].astype(F32)
        ).astype(BF)
        for d in range(2):
            start(rs_copy(op, c, 1, d), zpool)

    def ev_R5(c, op):
        rs_arrive(op, c, 4)
        part[op, c, z, :, theirs] = rs_total(op, c, theirs, theirs).astype(BF)
        start(rs_x(op, c), xpool)
        own[op, c] = rs_total(op, c, mine, mine)

    def ev_E(c, op):
        got = []
        for o in (PRE, GRAD):
            if RS_X[o][c]:
                rs_arrive(o, c, 4)
                got.append(rs_total(o, c, mine, pl.ds(0, half)))
            else:
                arrive(rs_x(o, c))
                got.append(own[o, c] + xland[o, c, 0].astype(F32))
        value, slope = gelu_both(got[PRE] + brow[0:1, :])
        full[PRE, c, z, :, mine] = value.astype(BF)
        full[GRAD, c, z, :, mine] = (got[GRAD] * slope).astype(BF)
        for o in (PRE, GRAD):
            if AG_X[o][c]:
                for d in range(2):
                    start(ag_copy(o, c, 1, d), zpool)
            start(ag_x(o, c, 0), xpool)

    def ev_A1(c, op):
        arrive(ag_x(op, c, 0))
        for d in range(2):
            start(ag_copy(op, c, 1, d), zpool)

    def ag_step(c, op, r):
        ag_arrive(op, c, r - 1)
        for d in range(2):
            start(ag_copy(op, c, r, d), zpool)
            if AG_X[op][c]:
                start(ag_x(op, c, (-SIGN[d] * (r - 1)) % NZ), xpool)

    def ev_A5(c, op):
        ag_arrive(op, c, 4)
        start(ag_x(op, c, 4), xpool)

    def ev_F1(c, op):
        if AG_X[op][c]:
            arrive_all(xland.at[op, c], axr.at[op, c])
        else:
            ag_arrive(op, c, 4)
        left = full[op, c].reshape(crow, width)
        v = dot_nn(left, wdn_vm[...]) if op == PRE else dot_nt(left, wup_vm[...])
        opart[c, op] = v.astype(BF).reshape(2, rows, feat)
        start(f_core(c, op), pool)

    def ev_F2(c, op):
        arrive(f_core(c, op))
        v = (opart[c, op, core].astype(F32) + rcore[c, op].astype(F32)).astype(BF)
        if CHUNKS[c][0]:
            sy[c, op] = v
            start(f_y(c, op), pool)
        else:
            ry[c, op] = v

    def ev_FX(c, op):
        sx[op] = ry_sum(1, op).astype(BF)
        start(f_xh(op), pool)

    def ev_W(c, op):
        p = c // 2
        acc, out, other = ((acc_u, gwu_vm, GRAD), (acc_d, None, PRE))[op]
        tct[op, p] = tc[op, c - 1:c + 1].reshape(2 * crow, feat).T

        @pl.loop(0, 3)
        def _(j):
            cols = pl.ds(pl.multiple_of(j * 512, 512), 512)
            v = dot_nn(tct[op, p], full[other, c - 1:c + 1, :, :, cols].reshape(2 * crow, 512))
            if p:
                v += acc[:, cols]
            if c == NC - 1 and op == PRE:
                gwu_vm[:, cols] = v.astype(BF)
            else:
                acc[:, cols] = v

        if c == NC - 1 and op == PRE:
            local(2).start()
        if c == NC - 1 and op == GRAD:
            gwd_vm[...] = acc_d[...].astype(BF).T
            local(3).start()

    def ev_C(c, op):
        v = full[GRAD, c - 1:c + 1].reshape(2 * crow // 8, 8, width).astype(F32)
        v = jnp.sum(v, axis=0)
        if c > 1:
            v += cs[...]
        cs[...] = v
        if c == NC - 1:
            piece = pl.ds(pl.multiple_of(lax.rem(gz, 4) * feat, 128), feat)
            bs[gy] = cs[:, piece]
            for d in (1, 2, 3):
                start(b_y(d), pool)

    def ev_D(c, op):
        gbd_vm[...] = jnp.sum(tc[1].reshape(NC * crow, feat).astype(F32), axis=0)
        local(11).start()

    def bias_step(r):
        if r == 1:
            arrive(bias_x())
        else:
            arrive_all(ball.at[0:2 if r < 5 else 1], bzr.at[r - 1])
        if r < 5:
            for d in range(2 if r < 4 else 1):
                start(bias_copy(r, d), zpool)
        else:
            for j in range(2):
                piece = gy * 4 + xl * 2 + j
                brow[:, j * feat:(j + 1) * feat] = ball[lax.rem(piece, NZ), lax.div(piece, NZ)]

    def ev_END(c, op):
        arrive_all(bs.at[0:3], hr.at[2 * NC])
        gbu_vm[...] = jnp.sum(bs[lax.div(gz, 4)], axis=0)
        local(10).start()
        for o in (PRE, GRAD):
            total = ry_sum(0, o)
            arrive(f_xh(o))
            total += rx[o].astype(F32)
            if o == PRE:
                out_vm[...] = (total + bdn_vm[...][None, :]).astype(BF)
            else:
                gtok_vm[...] = total.astype(BF)
            local(8 + o).start()

    events = {
        "H": ev_H, "HX": ev_HX, "HF": ev_HF, "PP": ev_PP, "R1": ev_R1, "R5": ev_R5,
        "E": ev_E, "A1": ev_A1, "A5": ev_A5, "F1": ev_F1, "F2": ev_F2, "FX": ev_FX,
        "W": ev_W, "C": ev_C, "D": ev_D, "END": ev_END,
    }

    def local(k):
        src, dst = (
            (wdn_hbm, wdn_vm), (wup_hbm, wup_vm), (gwu_vm, gwu_hbm), (gwd_vm, gwd_hbm),
            (tok_hbm, tc.at[0, 0, core]), (cot_hbm, tc.at[1, 0, core]),
            (bup_hbm, bup_vm), (bdn_hbm, bdn_vm), (out_vm, out_hbm), (gtok_vm, gtok_hbm),
            (gbu_vm, gbu_hbm), (gbd_vm, gbd_hbm),
        )[k]
        return pltpu.make_async_copy(src, dst, ls.at[k])

    for k in (4, 5, 6, 7, 0, 1):
        local(k).start()
    barrier = pltpu.get_barrier_semaphore()
    peers = (zdev[0], zdev[1], xdev, coredev, xhdev, ydev(1), ydev(2), ydev(3))
    for dev in peers:
        pl.semaphore_signal(barrier, inc=1, device_id=dev, device_id_type=MESH)
    for k in (4, 5, 6, 7):
        local(k).wait()
    ball[z, xl] = jnp.broadcast_to(bup_vm[...][None, :], ball.shape[2:])
    pl.semaphore_wait(barrier, len(peers))

    for kind, c, op in ORDER:
        if kind in ("R2", "R3", "R4"):
            rs_step(op, c, int(kind[1]))
        elif kind in ("A2", "A3", "A4"):
            ag_step(c, op, int(kind[1]))
        elif kind[0] == "B":
            bias_step(int(kind[1]))
        else:
            events[kind](c, op)
    for held, _ in slots.values():
        for copy in held:
            if copy is not None:
                copy.wait_send()
    for k in (2, 3, 8, 9, 10, 11):
        local(k).wait()


def hand_over(results):
    count = len(results)
    pieces = []
    for k, r in enumerate(results):
        parts = 4 if r.size > 2**18 else 1
        size = r.shape[0] // parts
        pieces += [(k, i * size, size) for i in range(parts)]

    def move(*refs):
        source, target, held = refs[:count], refs[count:2 * count], refs[2 * count:3 * count]
        sems = refs[3 * count]

        def copy(side, i):
            k, at, size = pieces[i]
            ends = (source[k], held[k], target[k])
            rows = pl.ds(at, size)
            return pltpu.make_async_copy(
                ends[side].at[rows], ends[side + 1].at[rows], sems.at[side, i]
            )

        for i in range(len(pieces)):
            copy(0, i).start()
        for i in range(len(pieces)):
            copy(0, i).wait()
            copy(1, i).start()
        for i in range(len(pieces)):
            copy(1, i).wait()

    place = pl.BlockSpec(memory_space=pl.ANY)
    return pl.pallas_call(
        move,
        out_shape=tuple(jax.ShapeDtypeStruct(r.shape, r.dtype) for r in results),
        in_specs=[place] * count,
        out_specs=(place,) * count,
        scratch_shapes=[pltpu.VMEM(r.shape, r.dtype) for r in results]
        + [pltpu.SemaphoreType.DMA((2, len(pieces)))],
        name="hand_over",
    )(*results)


def per_device(tokens, w_up, b_up, w_down, b_down, cotangent):
    rows, feat = tokens.shape
    width = w_up.shape[1]
    half = width // 2
    unit = 2 * rows // NZ
    place = pl.BlockSpec(memory_space=pl.ANY)
    dma = pltpu.SemaphoreType.DMA
    scratch = [
        pltpu.VMEM((2, NC, 2, rows, feat), BF),
        pltpu.VMEM((2, NC // 2, feat, 4 * rows), BF),
        pltpu.VMEM((2, NC, NZ, unit, width), BF),
        pltpu.VMEM((2, NC, 2, 4, unit, width), BF),
        pltpu.VMEM((2, NC, NZ, unit, half), BF),
        pltpu.VMEM((2, NC, unit, half), F32),
        pltpu.VMEM((2, NC, NZ, unit, width), BF),
        pltpu.VMEM((feat, width), F32),
        pltpu.VMEM((feat, width), F32),
        pltpu.VMEM((NC, 2, 2, rows, feat), BF),
        pltpu.VMEM((NC, 2, rows, feat), BF),
        pltpu.VMEM((NC, 2, rows, feat), BF),
        pltpu.VMEM((NC, 2, rows, feat), BF),
        pltpu.VMEM((2, rows, feat), BF),
        pltpu.VMEM((2, rows, feat), BF),
        pltpu.VMEM((8, width), F32),
        pltpu.VMEM((4, 8, feat), F32),
        pltpu.VMEM((NZ, 2, 8, feat), F32),
        pltpu.VMEM((8, half), F32),
        pltpu.VMEM((feat, width), BF),
        pltpu.VMEM((width, feat), BF),
        pltpu.VMEM((feat,), F32),
        pltpu.VMEM((feat,), F32),
        pltpu.VMEM((feat, width), BF),
        pltpu.VMEM((width, feat), BF),
        pltpu.VMEM((rows, feat), BF),
        pltpu.VMEM((rows, feat), BF),
        pltpu.VMEM((feat,), F32),
        pltpu.VMEM((feat,), F32),
        dma((2, NC, 2)),
        dma((2, NC)),
        dma((2, NC)),
        dma((2 * NC + 1,)),
        dma((2, 2, NC + 1)),
        dma((5,)),
        dma((Z_POOL,)),
        dma((X_POOL,)),
        dma((POOL,)),
        dma((12,)),
    ]
    results = pl.pallas_call(
        kernel,
        out_shape=(
            jax.ShapeDtypeStruct((rows, feat), BF),
            jax.ShapeDtypeStruct((rows, feat), BF),
            jax.ShapeDtypeStruct((feat, width), BF),
            jax.ShapeDtypeStruct((feat,), F32),
            jax.ShapeDtypeStruct((width, feat), BF),
            jax.ShapeDtypeStruct((feat,), F32),
        ),
        in_specs=[place] * 6,
        out_specs=(place,) * 6,
        scratch_shapes=scratch,
        compiler_params=pltpu.CompilerParams(
            collective_id=0, has_side_effects=True, vmem_limit_bytes=60 * 2**20
        ),
        name="mlp_block",
    )(tokens, w_up, b_up, w_down, b_down, cotangent)
    return hand_over(results)


def solution(mesh):
    rows = P(("gx", "gy"), "gz")
    up = P("gz", ("gx", "gy"))
    down = P(("gx", "gy"), "gz")
    return jax.shard_map(
        per_device,
        mesh=mesh,
        in_specs=(rows, up, P(("gx", "gz")), down, P("gz"), rows),
        out_specs=(rows, rows, up, P(("gx", "gz")), down, P("gz")),
        check_vma=False,
    )
```

```python
import jax
import jax.numpy as jnp
from jax import lax
from jax.experimental import pallas as pl
from jax.experimental.pallas import tpu as pltpu
from jax.sharding import PartitionSpec as P

BF = jnp.bfloat16
F32 = jnp.float32
MESH = pl.DeviceIdType.MESH
gelu_scale = 0.7978845608028654
gelu_cubic = 0.044715
NZ = 8
CHUNKS = ((0, 0), (1, 0), (1, 1), (2, 0), (2, 1), (3, 0), (3, 1), (0, 1))
NC = len(CHUNKS)
SIGN = (1, -1)
PRE, GRAD = 0, 1
Z_POOL, X_POOL, POOL = 20, 20, 12

RS_X = ((1, 1, 1, 0, 1, 1, 0, 1), (0, 0, 1, 0, 1, 0, 0, 1))
AG_X = ((1, 1, 1, 1, 0, 0, 1, 0), (1, 1, 0, 0, 1, 1, 0, 1))
ORDER = (
    ("H", 0, 0), ("PP", 0, 0), ("PP", 0, 1), ("HX", 0, 0), ("HF", 1, 0), ("B1", 0, 0),
    ("R2", 0, 1), ("PP", 7, 0), ("HF", 3, 0), ("PP", 1, 1), ("PP", 1, 0), ("B2", 0, 0),
    ("PP", 3, 0), ("R1", 0, 0), ("HF", 5, 0), ("R3", 0, 1), ("PP", 3, 1), ("HF", 2, 0),
    ("R2", 1, 1), ("B3", 0, 0), ("PP", 5, 1), ("R2", 3, 0), ("R2", 0, 0), ("HF", 4, 0),
    ("PP", 2, 0), ("R4", 0, 1), ("R2", 3, 1), ("R1", 7, 0), ("HF", 6, 0), ("R3", 1, 1),
    ("PP", 2, 1), ("B4", 0, 0), ("R2", 5, 1), ("PP", 4, 0), ("R3", 3, 0), ("R1", 1, 0),
    ("R3", 0, 0), ("PP", 4, 1), ("R5", 0, 1), ("PP", 5, 0), ("R3", 3, 1), ("R2", 7, 0),
    ("PP", 6, 0), ("B5", 0, 0), ("R4", 1, 1), ("R1", 2, 0), ("R3", 5, 1), ("PP", 7, 1),
    ("R4", 3, 0), ("R2", 1, 0), ("R4", 0, 0), ("PP", 6, 1), ("R4", 3, 1), ("D", 0, 0),
    ("R1", 2, 1), ("R2", 6, 0), ("R3", 7, 0), ("R5", 1, 1), ("R2", 2, 0), ("R4", 5, 1),
    ("R5", 3, 0), ("R1", 4, 0), ("R3", 1, 0), ("R2", 6, 1), ("R5", 3, 1), ("R2", 2, 1),
    ("R3", 6, 0), ("R4", 7, 0), ("R1", 4, 1), ("E", 0, 0), ("R3", 2, 0), ("R2", 4, 0),
    ("R5", 5, 1), ("R4", 1, 0), ("R3", 6, 1), ("R3", 2, 1), ("R4", 6, 0), ("R1", 5, 0),
    ("R2", 4, 1), ("A2", 0, 0), ("A2", 0, 1), ("R4", 2, 0), ("R3", 4, 0), ("R1", 7, 1),
    ("E", 1, 0), ("R4", 2, 1), ("E", 3, 0), ("R4", 6, 1), ("R3", 4, 1), ("A3", 0, 0),
    ("R2", 5, 0), ("A3", 0, 1), ("R5", 6, 0), ("R4", 4, 0), ("R2", 7, 1), ("A2", 1, 0),
    ("A2", 1, 1), ("E", 2, 0), ("A2", 3, 0), ("A1", 3, 1), ("R5", 6, 1), ("R4", 4, 1),
    ("A4", 0, 0), ("R3", 5, 0), ("A4", 0, 1), ("R3", 7, 1), ("A3", 1, 0), ("A3", 1, 1),
    ("A2", 2, 0), ("A3", 3, 0), ("A1", 2, 1), ("A2", 3, 1), ("E", 4, 0), ("A5", 0, 0),
    ("E", 6, 0), ("R4", 7, 1), ("A5", 0, 1), ("R4", 5, 0), ("A4", 1, 0), ("A4", 1, 1),
    ("A3", 2, 0), ("A4", 3, 0), ("A2", 2, 1), ("A3", 3, 1), ("A2", 4, 1), ("A2", 6, 0),
    ("A1", 4, 0), ("E", 7, 0), ("E", 5, 0), ("F1", 0, 0), ("A5", 1, 1), ("A5", 3, 0),
    ("A5", 1, 0), ("F1", 0, 1), ("A3", 2, 1), ("F2", 0, 0), ("A4", 2, 0), ("A1", 6, 1),
    ("A4", 3, 1), ("F2", 0, 1), ("A3", 4, 1), ("A3", 6, 0), ("A2", 4, 0), ("A2", 7, 1),
    ("A2", 5, 1), ("A4", 2, 1), ("A5", 2, 0), ("A1", 7, 0), ("A2", 6, 1), ("F1", 3, 1),
    ("A4", 4, 1), ("A1", 5, 0), ("A4", 6, 0), ("F1", 1, 1), ("C", 1, 0), ("A3", 4, 0),
    ("F1", 1, 0), ("A3", 7, 1), ("F1", 3, 0), ("F1", 2, 1), ("F2", 1, 0), ("C", 3, 0),
    ("A2", 7, 0), ("F2", 1, 1), ("F2", 3, 1), ("A3", 6, 1), ("F2", 2, 1), ("A5", 4, 1),
    ("F2", 3, 0), ("A3", 5, 1), ("W", 1, 1), ("A2", 5, 0), ("A5", 6, 0), ("W", 1, 0),
    ("A4", 4, 0), ("A4", 7, 1), ("F1", 2, 0), ("W", 3, 1), ("A3", 7, 0), ("W", 3, 0),
    ("A4", 5, 1), ("F2", 2, 0), ("A4", 6, 1), ("F1", 4, 1), ("A3", 5, 0), ("F1", 4, 0),
    ("A5", 7, 1), ("F1", 6, 0), ("F2", 4, 1), ("A4", 7, 0), ("A5", 5, 1), ("F2", 4, 0),
    ("F1", 6, 1), ("F2", 6, 0), ("A4", 5, 0), ("F1", 7, 1), ("F2", 6, 1), ("F1", 5, 1),
    ("C", 5, 0), ("F1", 7, 0), ("F2", 7, 1), ("C", 7, 0), ("F1", 5, 0), ("F2", 7, 0),
    ("FX", 0, 0), ("F2", 5, 1), ("W", 5, 0), ("FX", 0, 1), ("F2", 5, 0), ("W", 7, 0),
    ("W", 5, 1), ("W", 7, 1), ("END", 0, 0),
)


def gelu_both(v):
    t = jnp.tanh(gelu_scale * (v + gelu_cubic * v * v * v))
    value = 0.5 * v * (1.0 + t)
    slope = 0.5 * (1.0 + t) + 0.5 * v * (1.0 - t * t) * gelu_scale * (
        1.0 + 3.0 * gelu_cubic * v * v
    )
    return value, slope


def dot_nn(left, right):
    return jnp.dot(left, right, preferred_element_type=F32)


def dot_nt(left, right):
    return lax.dot_general(left, right, (((1,), (1,)), ((), ())), preferred_element_type=F32)


def kernel(
    tok_hbm, wup_hbm, bup_hbm, wdn_hbm, bdn_hbm, cot_hbm,
    out_hbm, gtok_hbm, gwu_hbm, gbu_hbm, gwd_hbm, gbd_hbm,
    tc, tct, part, zland, xland, own, full, acc_u, acc_d,
    opart, rcore, sy, ry, sx, rx, cs, bs, ball, brow,
    wup_vm, wdn_vm, bup_vm, bdn_vm, gwu_vm, gwd_vm,
    out_vm, gtok_vm, gbu_vm, gbd_vm,
    zr, rxr, axr, hr, fr, bzr, zpool, xpool, pool, ls,
):
    gx, gy, gz = lax.axis_index("gx"), lax.axis_index("gy"), lax.axis_index("gz")
    z, xl = lax.rem(gz, NZ), lax.div(gz, NZ)
    xh, core = lax.div(gx, 2), lax.rem(gx, 2)
    feat, width = wup_vm.shape
    half = width // 2
    rows = tok_hbm.shape[0]
    crow = 2 * rows
    unit = crow // NZ

    def zi(j):
        return lax.rem(z + j + NZ, NZ)

    def side(x, shift, size):
        return pl.ds(pl.multiple_of(x * half + shift, 128), size)

    mine, theirs = side(xl, 0, half), side(1 - xl, 0, half)
    zdev = ({"gz": xl * NZ + zi(1)}, {"gz": xl * NZ + zi(-1)})
    xdev = {"gz": (1 - xl) * NZ + z}
    coredev = {"gx": xh * 2 + 1 - core}
    xhdev = {"gx": (1 - xh) * 2 + core}

    def ydev(d):
        return {"gy": lax.rem(gy + d + 4, 4)}

    def rcopy(message, send_sem):
        src, dst, recv_sem, dev = message
        return pltpu.make_async_remote_copy(
            src_ref=src, dst_ref=dst, send_sem=send_sem, recv_sem=recv_sem,
            device_id=dev, device_id_type=MESH,
        )

    slots = {id(p): ([None] * p.shape[0], [0]) for p in (zpool, xpool, pool)}

    def start(message, sems):
        held, count = slots[id(sems)]
        k = count[0] % len(held)
        count[0] += 1
        if held[k] is not None:
            held[k].wait_send()
        held[k] = rcopy(message, sems.at[k])
        held[k].start()

    def arrive(message):
        rcopy(message, pool.at[0]).wait_recv()

    def arrive_all(like, sem):
        pltpu.make_async_copy(like, like, sem).wait()

    def rs_part(op, c, r, d):
        wide = half if RS_X[op][c] else width
        return (d * wide // 2, wide // 2) if r == 1 else (0, wide)

    def rs_unit(op, c, t, shift, size):
        cols = side(xl, shift, size) if RS_X[op][c] else pl.ds(shift, size)
        return part.at[op, c, t, :, cols]

    def rs_copy(op, c, r, d):
        shift, size = rs_part(op, c, r, d)
        return (
            rs_unit(op, c, zi(SIGN[d] * (5 - r)), shift, size),
            zland.at[op, c, d, r - 1, :, pl.ds(shift, size)],
            zr.at[op, c, r % 2], zdev[d],
        )

    def rs_arrive(op, c, r):
        wide = half if RS_X[op][c] else width
        like = zland.at[op, c, :, r - 1, :, pl.ds(0, wide // 2 if r == 1 else wide)]
        arrive_all(like, zr.at[op, c, r % 2])

    def rs_step(op, c, r):
        rs_arrive(op, c, r - 1)
        for d in range(2):
            shift, size = rs_part(op, c, r - 1, d)
            dst = rs_unit(op, c, zi(SIGN[d] * (5 - r)), shift, size)
            got = zland[op, c, d, r - 2, :, shift:shift + size]
            dst[...] = (dst[...].astype(F32) + got.astype(F32)).astype(BF)
            start(rs_copy(op, c, r, d), zpool)

    def rs_x(op, c):
        if RS_X[op][c]:
            src, dst = part.at[op, c, :, :, theirs], xland.at[op, c]
        else:
            src, dst = part.at[op, c, z, :, theirs], xland.at[op, c, 0]
        return src, dst, rxr.at[op, c], xdev

    def rs_total(op, c, cols, land):
        return (
            part[op, c, z, :, cols].astype(F32)
            + zland[op, c, 0, 3, :, land].astype(F32)
            + zland[op, c, 1, 3, :, land].astype(F32)
        )

    def ag_copy(op, c, r, d):
        t = zi(-SIGN[d] * (r - 1))
        wide = half if AG_X[op][c] else width
        shift, size = (d * wide // 2, wide // 2) if r == 4 else (0, wide)
        cols = side(xl, shift, size) if AG_X[op][c] else pl.ds(shift, size)
        ref = full.at[op, c, t, :, cols]
        return ref, ref, zr.at[op, c, r % 2], zdev[d]

    def ag_arrive(op, c, r):
        wide = half if AG_X[op][c] else width
        like = zland.at[op, c, :, 0, :, pl.ds(0, wide // 2 if r == 4 else wide)]
        arrive_all(like, zr.at[op, c, r % 2])

    def ag_x(op, c, j):
        ref = full.at[op, c, zi(j), :, mine]
        return ref, ref, axr.at[op, c], xdev

    def bias_x():
        return ball.at[z, xl], ball.at[z, xl], bzr.at[0], xdev

    def bias_copy(r, d):
        ref = ball.at[zi(-SIGN[d] * (r - 1))]
        return ref, ref, bzr.at[r], zdev[d]

    chunk_of = {pair: c for c, pair in enumerate(CHUNKS)}
    own_rows = tc.at[:, 0, core]
    last = chunk_of[(0, 1)]
    other_rows = tc.at[:, last, core]

    def h_copy(k, src, dst, dev):
        return src, dst, hr.at[k], dev

    def h_xh():
        return h_copy(0, own_rows, other_rows, xhdev)

    def h_y(c):
        u, h = CHUNKS[c]
        return h_copy(c, other_rows if h else own_rows, tc.at[:, c, core], ydev(-u))

    def h_core(c):
        ref = tc.at[:, c, core]
        return h_copy(NC + c, ref, ref, coredev)

    def f_core(c, op):
        return opart.at[c, op, 1 - core], rcore.at[c, op], fr.at[0, op, c], coredev

    def f_y(c, op):
        return sy.at[c, op], ry.at[c, op], fr.at[1, op, c], ydev(CHUNKS[c][0])

    def f_xh(op):
        return sx.at[op], rx.at[op], fr.at[0, op, NC], xhdev

    def ry_sum(h, op):
        picks = [c for c in range(NC) if CHUNKS[c][1] == h]
        for c in picks:
            if CHUNKS[c][0]:
                arrive(f_y(c, op))
        a, b, c, d = [ry[p, op].astype(F32) for p in picks]
        return (a + b) + (c + d)

    def b_y(d):
        return bs.at[gy], bs.at[gy], hr.at[2 * NC], ydev(d)

    def ev_H(c, op):
        start(h_core(0), pool)
        start(h_xh(), pool)
        for k in (1, 3, 5):
            start(h_y(k), pool)
        start(bias_x(), xpool)

    def ev_HX(c, op):
        arrive(h_xh())
        start(h_core(last), pool)
        for k in (2, 4, 6):
            start(h_y(k), pool)

    def ev_HF(c, op):
        arrive(h_y(c))
        start(h_core(c), pool)

    arrived = set()

    def ev_PP(c, op):
        if c not in arrived:
            arrived.add(c)
            arrive(h_core(c))
        if c == 0:
            local(0 if op == GRAD else 1).wait()
        x = tc[op, c].reshape(crow, feat)

        @pl.loop(0, 2)
        def _(j):
            cols = pl.ds(pl.multiple_of(j * half, half), half)
            v = dot_nt(x, wdn_vm[cols, :]) if op == GRAD else dot_nn(x, wup_vm[:, cols])
            part[op, c, :, :, cols] = v.astype(BF).reshape(NZ, unit, half)

        if RS_X[op][c]:
            start(rs_x(op, c), xpool)
        else:
            for d in range(2):
                start(rs_copy(op, c, 1, d), zpool)

    def ev_R1(c, op):
        arrive(rs_x(op, c))
        part[op, c, :, :, mine] = (
            part[op, c, :, :, mine].astype(F32) + xland[op, c].astype(F32)
        ).astype(BF)
        for d in range(2):
            start(rs_copy(op, c, 1, d), zpool)

    def ev_R5(c, op):
        rs_arrive(op, c, 4)
        part[op, c, z, :, theirs] = rs_total(op, c, theirs, theirs).astype(BF)
        start(rs_x(op, c), xpool)
        own[op, c] = rs_total(op, c, mine, mine)

    def ev_E(c, op):
        got = []
        for o in (PRE, GRAD):
            if RS_X[o][c]:
                rs_arrive(o, c, 4)
                got.append(rs_total(o, c, mine, pl.ds(0, half)))
            else:
                arrive(rs_x(o, c))
                got.append(own[o, c] + xland[o, c, 0].astype(F32))
        value, slope = gelu_both(got[PRE] + brow[...])
        full[PRE, c, z, :, mine] = value.astype(BF)
        full[GRAD, c, z, :, mine] = (got[GRAD] * slope).astype(BF)
        for o in (PRE, GRAD):
            if AG_X[o][c]:
                for d in range(2):
                    start(ag_copy(o, c, 1, d), zpool)
            start(ag_x(o, c, 0), xpool)

    def ev_A1(c, op):
        arrive(ag_x(op, c, 0))
        for d in range(2):
            start(ag_copy(op, c, 1, d), zpool)

    def ag_step(c, op, r):
        ag_arrive(op, c, r - 1)
        for d in range(2):
            start(ag_copy(op, c, r, d), zpool)
            if AG_X[op][c]:
                start(ag_x(op, c, (-SIGN[d] * (r - 1)) % NZ), xpool)

    def ev_A5(c, op):
        ag_arrive(op, c, 4)
        start(ag_x(op, c, 4), xpool)

    def ev_F1(c, op):
        if AG_X[op][c]:
            arrive_all(xland.at[op, c], axr.at[op, c])
        else:
            ag_arrive(op, c, 4)
        left = full[op, c].reshape(crow, width)
        v = dot_nn(left, wdn_vm[...]) if op == PRE else dot_nt(left, wup_vm[...])
        opart[c, op] = v.astype(BF).reshape(2, rows, feat)
        start(f_core(c, op), pool)

    def ev_F2(c, op):
        arrive(f_core(c, op))
        v = (opart[c, op, core].astype(F32) + rcore[c, op].astype(F32)).astype(BF)
        if CHUNKS[c][0]:
            sy[c, op] = v
            start(f_y(c, op), pool)
        else:
            ry[c, op] = v

    def ev_FX(c, op):
        sx[op] = ry_sum(1, op).astype(BF)
        start(f_xh(op), pool)

    def ev_W(c, op):
        p = c // 2
        acc, out, other = ((acc_u, gwu_vm, GRAD), (acc_d, None, PRE))[op]
        tct[op, p] = tc[op, c - 1:c + 1].reshape(2 * crow, feat).T

        @pl.loop(0, 3)
        def _(j):
            cols = pl.ds(pl.multiple_of(j * 512, 512), 512)
            v = dot_nn(tct[op, p], full[other, c - 1:c + 1, :, :, cols].reshape(2 * crow, 512))
            if p:
                v += acc[:, cols]
            if c == NC - 1 and op == PRE:
                gwu_vm[:, cols] = v.astype(BF)
            else:
                acc[:, cols] = v

        if c == NC - 1 and op == PRE:
            local(2).start()
        if c == NC - 1 and op == GRAD:
            gwd_vm[...] = acc_d[...].astype(BF).T
            local(3).start()

    def ev_C(c, op):
        v = full[GRAD, c - 1:c + 1].reshape(2 * crow // 8, 8, width).astype(F32)
        v = jnp.sum(v, axis=0)
        if c > 1:
            v += cs[...]
        cs[...] = v
        if c == NC - 1:
            piece = pl.ds(pl.multiple_of(lax.rem(gz, 4) * feat, 128), feat)
            bs[gy] = cs[:, piece]
            for d in (1, 2, 3):
                start(b_y(d), pool)

    def ev_D(c, op):
        gbd_vm[...] = jnp.sum(tc[1].reshape(NC * crow, feat).astype(F32), axis=0)
        local(11).start()

    def bias_step(r):
        if r == 1:
            arrive(bias_x())
        else:
            arrive_all(ball.at[0:2 if r < 5 else 1], bzr.at[r - 1])
        if r < 5:
            for d in range(2 if r < 4 else 1):
                start(bias_copy(r, d), zpool)
        else:
            for j in range(2):
                piece = gy * 4 + xl * 2 + j
                brow[:, j * feat:(j + 1) * feat] = ball[lax.rem(piece, NZ), lax.div(piece, NZ)]

    def ev_END(c, op):
        arrive_all(bs.at[0:3], hr.at[2 * NC])
        gbu_vm[...] = jnp.sum(bs[lax.div(gz, 4)], axis=0)
        local(10).start()
        for o in (PRE, GRAD):
            total = ry_sum(0, o)
            arrive(f_xh(o))
            total += rx[o].astype(F32)
            if o == PRE:
                out_vm[...] = (total + bdn_vm[...][None, :]).astype(BF)
            else:
                gtok_vm[...] = total.astype(BF)
            local(8 + o).start()

    events = {
        "H": ev_H, "HX": ev_HX, "HF": ev_HF, "PP": ev_PP, "R1": ev_R1, "R5": ev_R5,
        "E": ev_E, "A1": ev_A1, "A5": ev_A5, "F1": ev_F1, "F2": ev_F2, "FX": ev_FX,
        "W": ev_W, "C": ev_C, "D": ev_D, "END": ev_END,
    }

    def local(k):
        src, dst = (
            (wdn_hbm, wdn_vm), (wup_hbm, wup_vm), (gwu_vm, gwu_hbm), (gwd_vm, gwd_hbm),
            (tok_hbm, tc.at[0, 0, core]), (cot_hbm, tc.at[1, 0, core]),
            (bup_hbm, bup_vm), (bdn_hbm, bdn_vm), (out_vm, out_hbm), (gtok_vm, gtok_hbm),
            (gbu_vm, gbu_hbm), (gbd_vm, gbd_hbm),
        )[k]
        return pltpu.make_async_copy(src, dst, ls.at[k])

    barrier = pltpu.get_barrier_semaphore()
    peers = (zdev[0], zdev[1], xdev, coredev, xhdev, ydev(1), ydev(2), ydev(3))
    for dev in peers:
        pl.semaphore_signal(barrier, inc=1, device_id=dev, device_id_type=MESH)
    for k in (4, 5, 6, 7, 0, 1):
        local(k).start()
    for k in (4, 5, 6, 7):
        local(k).wait()
    ball[z, xl] = bup_vm[...][None, :]
    pl.semaphore_wait(barrier, len(peers))

    for kind, c, op in ORDER:
        if kind in ("R2", "R3", "R4"):
            rs_step(op, c, int(kind[1]))
        elif kind in ("A2", "A3", "A4"):
            ag_step(c, op, int(kind[1]))
        elif kind[0] == "B":
            bias_step(int(kind[1]))
        else:
            events[kind](c, op)
    for held, _ in slots.values():
        for copy in held:
            if copy is not None:
                copy.wait_send()
    for k in (2, 3, 8, 9, 10, 11):
        local(k).wait()


def hand_over(results):
    count = len(results)
    pieces = []
    for k, r in enumerate(results):
        parts = 4 if r.size > 2**18 else 1
        size = r.shape[0] // parts
        pieces += [(k, i * size, size) for i in range(parts)]

    def move(*refs):
        source, target, held = refs[:count], refs[count:2 * count], refs[2 * count:3 * count]
        sems = refs[3 * count]

        def copy(side, i):
            k, at, size = pieces[i]
            ends = (source[k], held[k], target[k])
            rows = pl.ds(at, size)
            return pltpu.make_async_copy(
                ends[side].at[rows], ends[side + 1].at[rows], sems.at[side, i]
            )

        for i in range(len(pieces)):
            copy(0, i).start()
        for i in range(len(pieces)):
            copy(0, i).wait()
            copy(1, i).start()
        for i in range(len(pieces)):
            copy(1, i).wait()

    place = pl.BlockSpec(memory_space=pl.ANY)
    return pl.pallas_call(
        move,
        out_shape=tuple(jax.ShapeDtypeStruct(r.shape, r.dtype) for r in results),
        in_specs=[place] * count,
        out_specs=(place,) * count,
        scratch_shapes=[pltpu.VMEM(r.shape, r.dtype) for r in results]
        + [pltpu.SemaphoreType.DMA((2, len(pieces)))],
        name="hand_over",
    )(*results)


def per_device(tokens, w_up, b_up, w_down, b_down, cotangent):
    rows, feat = tokens.shape
    width = w_up.shape[1]
    half = width // 2
    unit = 2 * rows // NZ
    place = pl.BlockSpec(memory_space=pl.ANY)
    dma = pltpu.SemaphoreType.DMA
    scratch = [
        pltpu.VMEM((2, NC, 2, rows, feat), BF),
        pltpu.VMEM((2, NC // 2, feat, 4 * rows), BF),
        pltpu.VMEM((2, NC, NZ, unit, width), BF),
        pltpu.VMEM((2, NC, 2, 4, unit, width), BF),
        pltpu.VMEM((2, NC, NZ, unit, half), BF),
        pltpu.VMEM((2, NC, unit, half), F32),
        pltpu.VMEM((2, NC, NZ, unit, width), BF),
        pltpu.VMEM((feat, width), F32),
        pltpu.VMEM((feat, width), F32),
        pltpu.VMEM((NC, 2, 2, rows, feat), BF),
        pltpu.VMEM((NC, 2, rows, feat), BF),
        pltpu.VMEM((NC, 2, rows, feat), BF),
        pltpu.VMEM((NC, 2, rows, feat), BF),
        pltpu.VMEM((2, rows, feat), BF),
        pltpu.VMEM((2, rows, feat), BF),
        pltpu.VMEM((8, width), F32),
        pltpu.VMEM((4, 8, feat), F32),
        pltpu.VMEM((NZ, 2, 1, feat), F32),
        pltpu.VMEM((1, half), F32),
        pltpu.VMEM((feat, width), BF),
        pltpu.VMEM((width, feat), BF),
        pltpu.VMEM((feat,), F32),
        pltpu.VMEM((feat,), F32),
        pltpu.VMEM((feat, width), BF),
        pltpu.VMEM((width, feat), BF),
        pltpu.VMEM((rows, feat), BF),
        pltpu.VMEM((rows, feat), BF),
        pltpu.VMEM((feat,), F32),
        pltpu.VMEM((feat,), F32),
        dma((2, NC, 2)),
        dma((2, NC)),
        dma((2, NC)),
        dma((2 * NC + 1,)),
        dma((2, 2, NC + 1)),
        dma((5,)),
        dma((Z_POOL,)),
        dma((X_POOL,)),
        dma((POOL,)),
        dma((12,)),
    ]
    results = pl.pallas_call(
        kernel,
        out_shape=(
            jax.ShapeDtypeStruct((rows, feat), BF),
            jax.ShapeDtypeStruct((rows, feat), BF),
            jax.ShapeDtypeStruct((feat, width), BF),
            jax.ShapeDtypeStruct((feat,), F32),
            jax.ShapeDtypeStruct((width, feat), BF),
            jax.ShapeDtypeStruct((feat,), F32),
        ),
        in_specs=[place] * 6,
        out_specs=(place,) * 6,
        scratch_shapes=scratch,
        compiler_params=pltpu.CompilerParams(
            collective_id=0, has_side_effects=True, vmem_limit_bytes=60 * 2**20
        ),
        name="mlp_block",
    )(tokens, w_up, b_up, w_down, b_down, cotangent)
    return hand_over(results)


def solution(mesh):
    rows = P(("gx", "gy"), "gz")
    up = P("gz", ("gx", "gy"))
    down = P(("gx", "gy"), "gz")
    return jax.shard_map(
        per_device,
        mesh=mesh,
        in_specs=(rows, up, P(("gx", "gz")), down, P("gz"), rows),
        out_specs=(rows, rows, up, P(("gx", "gz")), down, P("gz")),
        check_vma=False,
    )
```
